32 devices in a mesh: row: 4 (over z), col: 8 (over y, x, core).
Axes of the slice: x: 2, y: 2, z: 4, core: 2. Of those that a mesh axis runs over, the one named last changes fastest.
Arguments:
- slot_factors: bfloat16 [4, 8, 2, 1024, 256], P('row', 'col'), may hold values from -0.75 to 0.75
- slot_pairs: int32 [4, 8, 2], P('row', 'col'), may hold values from 0 to 2, as said below
- pivot_factors: bfloat16 [8, 1024, 256], P('row', 'col'), may hold values from -0.75 to 0.75
- a_factors: bfloat16 [8, 1024, 256], P('col'), as said below
- diag_factor: float32 [1024, 1024], replicated, as said below
- sketch: float32 [1024, 128], replicated, as said below
Outputs:
- panel_basis: float32 [8, 1024, 128], P('col')
- panel_coeff: float32 [8, 1024, 128], P('col')
The draws below stay inside these ranges and needn't reach their ends.
Inputs may be any that keep to these rules, and one draw needn't show every extreme that they name: `slot_pairs`: on each cell (r, c) the live codes come first, are distinct and below 2; the remaining entries equal 2. Every cell has at least one live slot, and in every draw some cell is full and some cell has exactly one. `diag_factor`: lower triangular; the diagonal lies between 1 and 2. `a_factors`: real values of order one. `sketch`: real values.
All inputs are finite; a program needn't handle non-finite values.
Results may differ from the reference program's by a relative error of at most 0.0003.
Values may be sent and summed in bfloat16 or wider, within the bound.
A program may use at most 64 MiB of HBM per device.

```python
import jax
import jax.numpy as jnp
from jax import lax

TILE = 1024
RANK = 128
TI = 1
TJ = 2
SLOTS = 2
ROWS_T = 8
COLS_T = 8
N_ROW = 4
N_COL = 8


def draw_slot_pairs(key, part):
    cell_total = N_ROW * N_COL
    key_count, key_perm = jax.random.split(jax.random.fold_in(key, 11))
    counts = jax.random.randint(key_count, (cell_total,), 1, SLOTS + 1)
    counts = counts.at[0].set(SLOTS).at[1].set(1)
    keys = jax.random.split(key_perm, cell_total)
    orderings = jax.vmap(lambda single: jax.random.permutation(single, TI * TJ))(keys)[:, :SLOTS]
    position = jnp.arange(SLOTS)
    pair_codes = jnp.where(position[None, :] < counts[:, None], orderings, TI * TJ)
    return pair_codes.reshape(N_ROW, N_COL, SLOTS).astype(jnp.int32)


def draw_diag_factor(key, part):
    key_below, key_diag = jax.random.split(jax.random.fold_in(key, 23))
    below_part = jax.random.normal(key_below, (TILE, TILE), jnp.float32) * (0.2 / jnp.sqrt(jnp.float32(TILE)))
    diagonal = jnp.exp(jax.random.uniform(key_diag, (TILE,), jnp.float32, 0.0, 0.693))
    factor = jnp.tril(below_part, -1) + jnp.diag(diagonal)
    return factor.astype(jnp.float32)


def joint_panel(key):
    key_sketch, key_left, key_noise = jax.random.split(jax.random.fold_in(key, 37), 3)
    root_tile = jnp.sqrt(jnp.float32(TILE))
    sketch_part = jax.random.normal(key_sketch, (TILE, RANK), jnp.float32) / root_tile
    left_part = jax.random.normal(key_left, (ROWS_T, TILE, RANK), jnp.float32) * 0.5
    noise_part = jax.random.normal(key_noise, (ROWS_T, TILE, RANK), jnp.float32) * 0.1
    right_part = 16.0 * sketch_part[None, :, :] + noise_part
    return (sketch_part, jnp.concatenate([left_part, right_part], axis=-1))


def draw_sketch(key, part):
    sketch_part, panel_part = joint_panel(key)
    return sketch_part.astype(jnp.float32)


def draw_a_factors(key, part):
    sketch_part, panel_part = joint_panel(key)
    return panel_part.astype(jnp.bfloat16)


def block_levels(key, extent, shards, smallest, largest):
    def one(dim, parts):
        draws = jax.random.uniform(jax.random.fold_in(jax.random.fold_in(key, 6), dim), (parts,), jnp.float32, smallest / len(shards), largest / len(shards))
        return jnp.repeat(jnp.exp(draws), extent[dim] // parts).reshape((-1,) + (1,) * (len(extent) - dim - 1))

    gain = one(*shards[0])
    for cut in shards[1:]:
        gain = gain * one(*cut)
    return gain


def scatter_about(key, dims, scale, bound, cuts=(), kind=jnp.bfloat16):
    level = block_levels(key, dims, cuts, -0.22, 0.18) if cuts else 1.0
    result = jax.random.normal(key, dims, jnp.float32) * scale * level
    return jnp.minimum(jnp.maximum(result, -bound), bound).astype(kind)


def setup_inputs(seed: int = 0) -> dict:
    arg_keys = jax.random.split(jax.random.key(seed), 7)
    slot_factors = scatter_about(arg_keys[0], (N_ROW, N_COL, SLOTS, TILE, 2 * RANK), 0.125, 0.75, ((0, 4), (1, 8)))
    slot_pairs = draw_slot_pairs(jax.random.fold_in(arg_keys[6], 71), 0)
    pivot_factors = scatter_about(arg_keys[2], (COLS_T, TILE, 2 * RANK), 0.125, 0.75, ((0, 4), (1, 8)))
    a_factors = draw_a_factors(jax.random.fold_in(arg_keys[6], 71), 0)
    diag_factor = draw_diag_factor(jax.random.fold_in(arg_keys[6], 71), 0)
    sketch = draw_sketch(jax.random.fold_in(arg_keys[6], 71), 0)
    return dict(slot_factors=slot_factors, slot_pairs=slot_pairs, pivot_factors=pivot_factors, a_factors=a_factors, diag_factor=diag_factor, sketch=sketch)


def orthonormal(sketch_rows):
    precise_mode = lax.Precision.HIGHEST
    gram_matrix = jnp.einsum('ibr,ibc->irc', sketch_rows, sketch_rows, precision=precise_mode)
    factor_low = jnp.linalg.cholesky(gram_matrix)
    solved = lax.linalg.triangular_solve(factor_low, jnp.swapaxes(sketch_rows, 1, 2), left_side=True, lower=True)
    return jnp.swapaxes(solved, 1, 2)

def slot_block(slot_factors, slot_pairs, row_index):
    block_data = lax.dynamic_index_in_dim(slot_factors, row_index, 0, keepdims=False).astype(jnp.float32)
    block_data = block_data.reshape(N_COL * SLOTS, TILE, 2 * RANK)
    pair_codes = lax.dynamic_index_in_dim(slot_pairs, row_index, 0, keepdims=False).reshape(-1)
    owner_col = jnp.repeat(jnp.arange(N_COL, dtype=jnp.int32), SLOTS)
    active_flag = pair_codes < TI * TJ
    tile_position = jnp.where(active_flag, owner_col * TI + pair_codes // TJ, 0).astype(jnp.int32)
    column_position = (row_index * TJ + pair_codes % TJ).astype(jnp.int32)
    return (block_data[..., :RANK], block_data[..., RANK:], tile_position, column_position, active_flag.astype(jnp.float32))

def reference(slot_factors, slot_pairs, pivot_factors, a_factors, diag_factor, sketch):
    precise_mode = lax.Precision.HIGHEST
    pivot_data = pivot_factors.astype(jnp.float32)
    pivot_left_factor = pivot_data[..., :RANK]
    pivot_right_factor = pivot_data[..., RANK:]
    weights = jnp.einsum('jbr,bc->jrc', pivot_left_factor, sketch, precision=precise_mode)
    a_data = a_factors.astype(jnp.float32)
    a_left = a_data[..., :RANK]
    a_right = a_data[..., RANK:]
    a_sketch = jnp.einsum('ibr,bc->irc', a_right, sketch, precision=precise_mode)
    y_a = jnp.einsum('ibr,irc->ibc', a_left, a_sketch, precision=precise_mode)

    def first_pass(row_index, totals):
        slot_left_factor, slot_right_factor, tile_position, column_position, active_flag = slot_block(slot_factors, slot_pairs, row_index)
        coupling_matrix = jnp.einsum('jzk,jzu->jku', slot_right_factor, pivot_right_factor[column_position], precision=precise_mode)
        panel_kernel = jnp.einsum('src,scd->srd', coupling_matrix, weights[column_position], precision=precise_mode)
        update_contribution = jnp.einsum('gxn,gny->gxy', slot_left_factor, panel_kernel, precision=precise_mode) * active_flag[:, None, None]
        return totals.at[tile_position].add(update_contribution)
    zeros = jnp.zeros((ROWS_T, TILE, RANK), jnp.float32)
    y_sum = lax.fori_loop(0, N_ROW, first_pass, zeros)
    basis_column_count = orthonormal(y_a - y_sum)

    def second_pass(row_index, totals):
        slot_left_factor, slot_right_factor, tile_position, column_position, active_flag = slot_block(slot_factors, slot_pairs, row_index)
        coupling_matrix = jnp.einsum('jzk,jzu->jku', slot_right_factor, pivot_right_factor[column_position], precision=precise_mode)
        inner_product = jnp.einsum('jzk,jzu->jku', slot_left_factor, basis_column_count[tile_position], precision=precise_mode)
        reduced = jnp.einsum('src,srd->scd', coupling_matrix, inner_product, precision=precise_mode)
        lifted = jnp.einsum('sbc,scd->sbd', pivot_left_factor[column_position], reduced, precision=precise_mode)
        return totals.at[tile_position].add(lifted * active_flag[:, None, None])
    m_sum = lax.fori_loop(0, N_ROW, second_pass, zeros)
    m_a = jnp.einsum('ibr,irc->ibc', a_right, jnp.einsum('ibr,ibc->irc', a_left, basis_column_count, precision=precise_mode), precision=precise_mode)
    projected = m_a - m_sum
    stacked = jnp.transpose(projected, (1, 0, 2)).reshape(TILE, ROWS_T * RANK)
    solved = lax.linalg.triangular_solve(diag_factor, stacked, left_side=True, lower=True)
    coefficient = jnp.transpose(solved.reshape(TILE, ROWS_T, RANK), (1, 0, 2))
    root_tile = jnp.sqrt(jnp.float32(TILE))
    return (basis_column_count * root_tile, coefficient / root_tile)
```

```python
import functools

import jax
import jax.numpy as jnp
from jax import lax
from jax.experimental import pallas as pl
from jax.experimental.pallas import tpu as pltpu
from jax.sharding import PartitionSpec as P

MESH = pl.DeviceIdType.MESH
F32 = jnp.float32
BF16 = jnp.bfloat16
NN = (((1,), (0,)), ((), ()))
TN = (((0,), (0,)), ((), ()))
NT = (((1,), (1,)), ((), ()))


def split(x):
    high = x.astype(BF16)
    return high, (x - high.astype(F32)).astype(BF16)


def dot(a, b, dims=NN):
    return lax.dot_general(a, b, dims, preferred_element_type=F32)


def dot_exact_left(a, b, dims=NN):
    high, low = split(b)
    return dot(a, high, dims) + dot(a, low, dims)


def dot_split(a, b, dims=NN):
    a_high, a_low = a
    b_high, b_low = b
    return dot(a_high, b_high, dims) + (dot(a_high, b_low, dims) + dot(a_low, b_high, dims))


def dot_wide(a, b, dims=NN):
    return dot_split(split(a), split(b), dims)


def kernel(
    n_row, n_col,
    slot_ref, pairs_ref, pivot_ref, a_ref, diag_ref, sketch_ref,
    basis_ref, coeff_ref,
    diag_v, inv_small, inv_high, inv_low, pv_all, pu_all, coupling,
    y_own, y_part, y_in, y_full, x_all, hinv,
    diag_sem, pv_send, pv_recv, pu_send, pu_recv, pz_send, pz_recv,
    pf_send, pf_recv, rs_send, rs_recv, ag_send, ag_recv, x_send, x_recv,
):
    tile, rank = sketch_ref.shape
    columns, rows = pivot_ref.shape[0], pivot_ref.shape[1]
    slots = slot_ref.shape[2]
    chunk = tile // n_row
    r = lax.axis_index("row")
    c = lax.axis_index("col")

    diag_copy = pltpu.make_async_copy(diag_ref, diag_v, diag_sem)
    diag_copy.start()

    def piece(index):
        return pl.ds(pl.multiple_of(index * rows, rows), rows)

    def part(index):
        return pl.ds(pl.multiple_of(index * chunk, chunk), chunk)

    for j in range(columns):
        lanes = slice(j * rank, (j + 1) * rank)
        pu_all[r, piece(c), lanes] = pivot_ref[j, :, :rank]
        pv_all[piece(c), lanes] = pivot_ref[j, :, rank:]

    barrier = pltpu.get_barrier_semaphore()

    def greet_col(d, _):
        pl.semaphore_signal(barrier, inc=1, device_id={"col": lax.rem(c + d, n_col)}, device_id_type=MESH)
        return 0

    def greet_row(d, _):
        pl.semaphore_signal(barrier, inc=1, device_id={"row": lax.rem(r + d, n_row)}, device_id_type=MESH)
        return 0

    lax.fori_loop(1, n_col, greet_col, 0)
    lax.fori_loop(1, n_row, greet_row, 0)
    pl.semaphore_wait(barrier, n_col - 1 + n_row - 1)

    def to_col(ref, send, recv, d):
        return pltpu.make_async_remote_copy(
            ref, ref, send, recv, device_id={"col": lax.rem(c + d, n_col)}, device_id_type=MESH
        )

    def to_row(source, target, send, recv, d):
        return pltpu.make_async_remote_copy(
            source, target, send, recv, device_id={"row": lax.rem(r + d, n_row)}, device_id_type=MESH
        )

    def pv_copy(d, index):
        return to_col(pv_all.at[piece(index)], pv_send.at[d - 1], pv_recv.at[d - 1], d)

    def pu_copy(d, index):
        return to_col(pu_all.at[r, piece(index)], pu_send.at[d - 1], pu_recv.at[d - 1], d)

    def pz_copy(d, index):
        ref = pu_all.at[index, piece(c)]
        return to_row(ref, ref, pz_send.at[d - 1], pz_recv.at[d - 1], d)

    def pf_copy(e, d, index):
        from_row = lax.rem(r + n_row - e, n_row)
        return to_col(
            pu_all.at[from_row, piece(index)], pf_send.at[e - 1, d - 1], pf_recv.at[e - 1, d - 1], d
        )

    def rs_copy(d):
        return to_row(
            y_part.at[part(lax.rem(r + d, n_row))], y_in.at[d - 1], rs_send.at[d - 1], rs_recv.at[d - 1], d
        )

    def ag_copy(d, index):
        ref = y_full.at[part(index)]
        return to_row(ref, ref, ag_send.at[d - 1], ag_recv.at[d - 1], d)

    def x_copy(d, index):
        ref = x_all.at[index]
        return to_row(ref, ref, x_send.at[d - 1], x_recv.at[d - 1], d)

    def col_source(d):
        return lax.rem(c + n_col - d, n_col)

    def row_source(d):
        return lax.rem(r + n_row - d, n_row)

    def each(n, act):
        def body(d, _):
            act(d)
            return 0

        lax.fori_loop(1, n, body, 0)

    def push_pivots(d):
        pv_copy(d, c).start()
        pu_copy(d, c).start()

    each(n_col, push_pivots)
    each(n_row, lambda d: pz_copy(d, r).start())

    sketch_split = split(sketch_ref[...])
    a_left = a_ref[0, :, :rank]
    a_right = a_ref[0, :, rank:]
    a_sketch = dot(a_right, sketch_split[0], TN) + dot(a_right, sketch_split[1], TN)
    y_own[...] = dot_exact_left(a_left, a_sketch)

    diag_copy.wait()
    blocks = tile // rank
    sub = lax.broadcasted_iota(jnp.int32, (rank, rank), 0)
    lane = lax.broadcasted_iota(jnp.int32, (rank, rank), 1)
    on_diag = sub == lane

    def diag_block(b):
        span = slice(b * rank, (b + 1) * rank)
        return diag_v[span, span]

    for b in range(blocks):
        low = diag_block(b)
        only = jnp.where(on_diag, low, 0.0)
        inv_sub = 1.0 / jnp.sum(only, axis=1, keepdims=True)
        inv_lane = 1.0 / jnp.sum(only, axis=0, keepdims=True)
        pair = (sub == lane + 1) & ((lane & 1) == 0)
        inv_small[b] = jnp.where(on_diag, inv_lane, 0.0) - jnp.where(pair, low * inv_sub * inv_lane, 0.0)

    def double(level, _):
        step = (lax.shift_right_logical(sub, level + 1) == lax.shift_right_logical(lane, level + 1)) & (
            lax.shift_right_logical(sub, level) != lax.shift_right_logical(lane, level)
        )
        for b in range(blocks):
            now = inv_small[b]
            now_split = split(now)
            cross = split(jnp.where(step, diag_block(b), 0.0))
            inv_small[b] = now - dot_split(split(dot_split(now_split, cross)), now_split)
        return 0

    lax.fori_loop(1, rank.bit_length() - 1, double, 0)

    each(n_col, lambda d: pv_copy(d, col_source(d)).wait_recv())
    each(n_col, lambda d: pu_copy(d, col_source(d)).wait_recv())
    pivot_right = pv_all[...]
    for s in range(slots):
        code = pairs_ref[0, 0, s]
        coupled = dot(slot_ref[0, 0, s, :, rank:], pivot_right, TN)
        for j in range(columns):
            lanes = slice(j * rank, (j + 1) * rank)
            coupling[s * rank:(s + 1) * rank, lanes] = jnp.where(code == j, coupled[:, lanes], 0.0)
    pivot_left = pu_all[r]
    weights = dot(pivot_left, sketch_split[0], TN) + dot(pivot_left, sketch_split[1], TN)
    mixed = dot_wide(coupling[...], weights)
    total = dot_exact_left(slot_ref[0, 0, 0, :, :rank], mixed[:rank])
    for s in range(1, slots):
        total += dot_exact_left(slot_ref[0, 0, s, :, :rank], mixed[s * rank:(s + 1) * rank])
    y_part[...] = total
    each(n_row, lambda d: rs_copy(d).start())

    def forward(e):
        pz_copy(e, row_source(e)).wait_recv()
        each(n_col, lambda d: pf_copy(e, d, c).start())

    each(n_row, forward)

    inv_high[...] = jnp.zeros_like(inv_high)
    inv_low[...] = jnp.zeros_like(inv_low)
    for b in range(blocks):
        span = slice(b * rank, (b + 1) * rank)
        high, low = split(inv_small[b])
        inv_high[span, span] = high
        inv_low[span, span] = low
    size = rank
    while size < tile:
        for start in range(0, tile, 2 * size):
            first = slice(start, start + size)
            second = slice(start + size, start + 2 * size)
            middle = dot_split(split(diag_v[second, first]), (inv_high[first, first], inv_low[first, first]))
            cross = dot_split((inv_high[second, second], inv_low[second, second]), split(middle))
            high, low = split(-cross)
            inv_high[second, first] = high
            inv_low[second, first] = low
        size *= 2

    each(n_row, lambda d: rs_copy(d).wait_recv())
    mine = y_own[part(r)] - y_part[part(r)]
    for d in range(1, n_row):
        mine = mine - y_in[d - 1]
    y_full[part(r)] = mine
    each(n_row, lambda d: ag_copy(d, r).start())
    each(n_row, lambda d: ag_copy(d, row_source(d)).wait_recv())

    sketched = y_full[...]
    sketched_split = split(sketched)
    gram = lax.dot_general(sketched, sketched, TN, precision=lax.Precision.HIGHEST, preferred_element_type=F32)
    state = jnp.concatenate([gram, jnp.where(on_diag, 1.0, 0.0)], axis=1)
    group = 8
    sub_group = lax.broadcasted_iota(jnp.int32, (group, 1), 0)
    lane_group = lax.broadcasted_iota(jnp.int32, (group, 2 * rank), 1)
    sub_wide = lax.broadcasted_iota(jnp.int32, (group, 2 * rank), 0)
    for start in range(0, rank, group):
        block = state[start:start + group]
        for t in range(group - 1):
            k = start + t
            factor = block[:, k:k + 1] / block[t:t + 1, k:k + 1]
            block = block - jnp.where(sub_group > t, factor, 0.0) * block[t:t + 1]
        pivots = jnp.sum(jnp.where(lane_group == sub_wide + start, block, 0.0), axis=1, keepdims=True)
        block = block * lax.rsqrt(pivots)
        hinv[start:start + group] = block[:, rank:]
        if start + group < rank:
            left = jnp.where(lane_group[:, :rank] >= start + group, block[:, :rank], 0.0)
            state = state - dot_wide(left, block, TN)

    basis_split = split(dot_split(sketched_split, split(hinv[...]), NT))
    basis = basis_split[0].astype(F32) + basis_split[1].astype(F32)

    def across(left):
        return dot(left, basis_split[0], TN) + dot(left, basis_split[1], TN)

    inner = jnp.concatenate([across(slot_ref[0, 0, s, :, :rank]) for s in range(slots)], axis=0)
    x_all[r] = dot_wide(coupling[...], inner, TN)
    each(n_row, lambda d: x_copy(d, r).start())

    root = float(tile) ** 0.5
    basis_ref[0] = basis * root
    projected = dot_exact_left(a_right, across(a_left))
    each(n_row, lambda e: each(n_col, lambda d: pf_copy(e, d, col_source(d)).wait_recv()))
    each(n_row, lambda d: x_copy(d, row_source(d)).wait_recv())
    for row in range(n_row):
        projected = projected - dot_exact_left(pu_all[row], x_all[row])
    projected_split = split(projected)
    coeff_ref[0] = dot_split((inv_high[...], inv_low[...]), projected_split) * (1.0 / root)

    def finish_col(d):
        pv_copy(d, c).wait_send()
        pu_copy(d, c).wait_send()

    def finish_row(d):
        pz_copy(d, r).wait_send()
        rs_copy(d).wait_send()
        ag_copy(d, r).wait_send()
        x_copy(d, r).wait_send()

    each(n_col, finish_col)
    each(n_row, finish_row)
    each(n_row, lambda e: each(n_col, lambda d: pf_copy(e, d, c).wait_send()))


def solution(mesh):
    n_row, n_col = mesh.shape["row"], mesh.shape["col"]

    def shards(slot_factors, slot_pairs, pivot_factors, a_factors, diag_factor, sketch):
        tile, rank = sketch.shape
        columns, rows = pivot_factors.shape[:2]
        slots = slot_factors.shape[2]
        chunk = tile // n_row
        vmem = pl.BlockSpec(memory_space=pltpu.VMEM)
        dma = pltpu.SemaphoreType.DMA
        out = jax.ShapeDtypeStruct((1, tile, rank), F32)
        return pl.pallas_call(
            functools.partial(kernel, n_row, n_col),
            out_shape=(out, out),
            in_specs=[vmem, pl.BlockSpec(memory_space=pltpu.SMEM), vmem, vmem, pl.BlockSpec(memory_space=pl.ANY), vmem],
            out_specs=(vmem, vmem),
            scratch_shapes=[
                pltpu.VMEM((tile, tile), F32),
                pltpu.VMEM((tile // rank, rank, rank), F32),
                pltpu.VMEM((tile, tile), BF16),
                pltpu.VMEM((tile, tile), BF16),
                pltpu.VMEM((tile, columns * rank), BF16),
                pltpu.VMEM((n_row, tile, columns * rank), BF16),
                pltpu.VMEM((slots * rank, columns * rank), F32),
                pltpu.VMEM((tile, rank), F32),
                pltpu.VMEM((tile, rank), F32),
                pltpu.VMEM((n_row - 1, chunk, rank), F32),
                pltpu.VMEM((tile, rank), F32),
                pltpu.VMEM((n_row, columns * rank, rank), F32),
                pltpu.VMEM((rank, rank), F32),
                dma(()),
                dma((n_col - 1,)), dma((n_col - 1,)),
                dma((n_col - 1,)), dma((n_col - 1,)),
                dma((n_row - 1,)), dma((n_row - 1,)),
                dma((n_row - 1, n_col - 1)), dma((n_row - 1, n_col - 1)),
                dma((n_row - 1,)), dma((n_row - 1,)),
                dma((n_row - 1,)), dma((n_row - 1,)),
                dma((n_row - 1,)), dma((n_row - 1,)),
            ],
            compiler_params=pltpu.CompilerParams(
                collective_id=0, has_side_effects=True, vmem_limit_bytes=56 * 1024 * 1024
            ),
            cost_estimate=pl.CostEstimate(flops=4 * 10**9, bytes_accessed=8 * 10**6, transcendentals=0),
        )(slot_factors, slot_pairs, pivot_factors, a_factors, diag_factor, sketch)

    in_specs = (
        P("row", "col", None, None, None),
        P("row", "col", None),
        P("row", "col", None),
        P("col", None, None),
        P(),
        P(),
    )
    out_specs = (P("col", None, None), P("col", None, None))
    return jax.shard_map(shards, mesh=mesh, in_specs=in_specs, out_specs=out_specs, check_vma=False)
```

```python
import functools

import jax
import jax.numpy as jnp
from jax import lax
from jax.experimental import pallas as pl
from jax.experimental.pallas import tpu as pltpu
from jax.sharding import PartitionSpec as P

MESH = pl.DeviceIdType.MESH
F32 = jnp.float32
BF16 = jnp.bfloat16
NN = (((1,), (0,)), ((), ()))
TN = (((0,), (0,)), ((), ()))
NT = (((1,), (1,)), ((), ()))


def split(x):
    high = x.astype(BF16)
    return high, (x - high.astype(F32)).astype(BF16)


def dot(a, b, dims=NN):
    return lax.dot_general(a, b, dims, preferred_element_type=F32)


def dot_exact_left(a, b, dims=NN):
    high, low = split(b)
    return dot(a, high, dims) + dot(a, low, dims)


def dot_split(a, b, dims=NN):
    a_high, a_low = a
    b_high, b_low = b
    return dot(a_high, b_high, dims) + (dot(a_high, b_low, dims) + dot(a_low, b_high, dims))


def dot_wide(a, b, dims=NN):
    return dot_split(split(a), split(b), dims)


def kernel(
    n_row, n_col,
    slot_ref, pairs_ref, pivot_ref, a_ref, diag_ref, sketch_ref,
    sketched_ref, solved_ref, hinv_ref,
    diag_v, inv_small, inv_high, inv_low, pv_all, pu_all, coupling,
    y_own, y_part, y_in, y_full, x_all,
    diag_sem, pv_send, pv_recv, pu_send, pu_recv, sv_send, sv_recv, su_send, su_recv, pz_send, pz_recv,
    pf_send, pf_recv, sf_send, sf_recv, rs_send, rs_recv, ag_send, ag_recv, x_send, x_recv,
):
    tile, rank = sketch_ref.shape
    columns, rows = pivot_ref.shape[0], pivot_ref.shape[1]
    slots = slot_ref.shape[2]
    chunk = tile // n_row
    r = lax.axis_index("row")
    c = lax.axis_index("col")
    n_chip = n_col // 2
    core, chip = lax.rem(c, 2), lax.div(c, 2)
    sibling = c + 1 - 2 * core

    diag_copy = pltpu.make_async_copy(diag_ref, diag_v, diag_sem)
    diag_copy.start()

    def piece(index):
        return pl.ds(pl.multiple_of(index * rows, rows), rows)

    def part(index):
        return pl.ds(pl.multiple_of(index * chunk, chunk), chunk)

    for j in range(columns):
        lanes = slice(j * rank, (j + 1) * rank)
        pu_all[r, piece(c), lanes] = pivot_ref[j, :, :rank]
        pv_all[piece(c), lanes] = pivot_ref[j, :, rank:]

    barrier = pltpu.get_barrier_semaphore()

    def chip_mate(e):
        return lax.rem(chip + e, n_chip) * 2 + core

    def chip_source(e):
        return lax.rem(chip + n_chip - e, n_chip) * 2 + core

    def sibling_source(e):
        return lax.rem(chip + n_chip - e, n_chip) * 2 + 1 - core

    def greet_chip(e, _):
        pl.semaphore_signal(barrier, inc=1, device_id={"col": chip_mate(e)}, device_id_type=MESH)
        return 0

    def greet_row(d, _):
        pl.semaphore_signal(barrier, inc=1, device_id={"row": lax.rem(r + d, n_row)}, device_id_type=MESH)
        return 0

    lax.fori_loop(1, n_chip, greet_chip, 0)
    lax.fori_loop(1, n_row, greet_row, 0)
    pl.semaphore_signal(barrier, inc=1, device_id={"col": sibling}, device_id_type=MESH)
    pl.semaphore_wait(barrier, n_chip - 1 + n_row - 1 + 1)

    def to_col(ref, send, recv, target):
        return pltpu.make_async_remote_copy(
            ref, ref, send, recv, device_id={"col": target}, device_id_type=MESH
        )

    def to_row(source, target, send, recv, d):
        return pltpu.make_async_remote_copy(
            source, target, send, recv, device_id={"row": lax.rem(r + d, n_row)}, device_id_type=MESH
        )

    def pv_copy(e, index):
        return to_col(pv_all.at[piece(index)], pv_send.at[e - 1], pv_recv.at[e - 1], chip_mate(e))

    def pu_copy(e, index):
        return to_col(pu_all.at[r, piece(index)], pu_send.at[e - 1], pu_recv.at[e - 1], chip_mate(e))

    def sv_copy(e, index):
        return to_col(pv_all.at[piece(index)], sv_send.at[e], sv_recv.at[e], sibling)

    def su_copy(e, index):
        return to_col(pu_all.at[r, piece(index)], su_send.at[e], su_recv.at[e], sibling)

    def pz_copy(d, index):
        ref = pu_all.at[index, piece(c)]
        return to_row(ref, ref, pz_send.at[d - 1], pz_recv.at[d - 1], d)

    def pf_copy(d, e, index):
        ref = pu_all.at[row_source(d), piece(index)]
        return to_col(ref, pf_send.at[d - 1, e - 1], pf_recv.at[d - 1, e - 1], chip_mate(e))

    def sf_copy(d, e, index):
        ref = pu_all.at[row_source(d), piece(index)]
        return to_col(ref, sf_send.at[d - 1, e], sf_recv.at[d - 1, e], sibling)

    def rs_copy(d):
        return to_row(
            y_part.at[part(lax.rem(r + d, n_row))], y_in.at[d - 1], rs_send.at[d - 1], rs_recv.at[d - 1], d
        )

    def ag_copy(d, index):
        ref = y_full.at[part(index)]
        return to_row(ref, ref, ag_send.at[d - 1], ag_recv.at[d - 1], d)

    def x_copy(d, index):
        ref = x_all.at[index]
        return to_row(ref, ref, x_send.at[d - 1], x_recv.at[d - 1], d)

    def row_source(d):
        return lax.rem(r + n_row - d, n_row)

    def each(n, act):
        def body(d, _):
            act(d)
            return 0

        lax.fori_loop(1, n, body, 0)

    def push_pivots(e):
        pv_copy(e, c).start()
        pu_copy(e, c).start()

    each(n_chip, push_pivots)
    sv_copy(0, c).start()
    su_copy(0, c).start()
    each(n_row, lambda d: pz_copy(d, r).start())

    sketch_split = split(sketch_ref[...])
    a_left = a_ref[0, :, :rank]
    a_right = a_ref[0, :, rank:]
    a_sketch = dot(a_right, sketch_split[0], TN) + dot(a_right, sketch_split[1], TN)
    y_own[...] = dot_exact_left(a_left, a_sketch)

    def pass_pivots(e):
        pv_copy(e, chip_source(e)).wait_recv()
        sv_copy(e, chip_source(e)).start()
        pu_copy(e, chip_source(e)).wait_recv()
        su_copy(e, chip_source(e)).start()

    diag_copy.wait()
    blocks = tile // rank
    sub = lax.broadcasted_iota(jnp.int32, (rank, rank), 0)
    lane = lax.broadcasted_iota(jnp.int32, (rank, rank), 1)
    on_diag = sub == lane

    def diag_block(b):
        span = slice(b * rank, (b + 1) * rank)
        return diag_v[span, span]

    for b in range(blocks):
        low = diag_block(b)
        only = jnp.where(on_diag, low, 0.0)
        inv_sub = 1.0 / jnp.sum(only, axis=1, keepdims=True)
        inv_lane = 1.0 / jnp.sum(only, axis=0, keepdims=True)
        pair = (sub == lane + 1) & ((lane & 1) == 0)
        inv_small[b] = jnp.where(on_diag, inv_lane, 0.0) - jnp.where(pair, low * inv_sub * inv_lane, 0.0)

    def double(level, _):
        step = (lax.shift_right_logical(sub, level + 1) == lax.shift_right_logical(lane, level + 1)) & (
            lax.shift_right_logical(sub, level) != lax.shift_right_logical(lane, level)
        )
        for b in range(blocks):
            now = inv_small[b]
            now_split = split(now)
            cross = split(jnp.where(step, diag_block(b), 0.0))
            inv_small[b] = now - dot_split(split(dot_split(now_split, cross)), now_split)
        return 0

    levels = rank.bit_length() - 1
    lax.fori_loop(1, levels // 2 + 1, double, 0)
    each(n_chip, pass_pivots)
    lax.fori_loop(levels // 2 + 1, levels, double, 0)

    def take_pivots(e):
        sv_copy(e, sibling_source(e)).wait_recv()
        su_copy(e, sibling_source(e)).wait_recv()

    take_pivots(0)
    each(n_chip, take_pivots)
    pivot_right = pv_all[...]
    for s in range(slots):
        code = pairs_ref[0, 0, s]
        coupled = dot(slot_ref[0, 0, s, :, rank:], pivot_right, TN)
        for j in range(columns):
            lanes = slice(j * rank, (j + 1) * rank)
            coupling[s * rank:(s + 1) * rank, lanes] = jnp.where(code == j, coupled[:, lanes], 0.0)
    pivot_left = pu_all[r]
    weights = dot(pivot_left, sketch_split[0], TN) + dot(pivot_left, sketch_split[1], TN)
    mixed = dot_wide(coupling[...], weights)
    mixed_split = split(mixed)

    def update_rows(index):
        span = part(index)
        total = jnp.zeros((chunk, rank), F32)
        for s in range(slots):
            left = slot_ref[0, 0, s, span, :rank]
            for half in mixed_split:
                total += dot(left, half[s * rank:(s + 1) * rank])
        y_part[span] = total

    def push_update(d):
        update_rows(lax.rem(r + d, n_row))
        rs_copy(d).start()

    each(n_row, push_update)
    update_rows(r)

    def forward(d):
        pz_copy(d, row_source(d)).wait_recv()
        each(n_chip, lambda e: pf_copy(d, e, c).start())
        sf_copy(d, 0, c).start()

    each(n_row, forward)

    inv_high[...] = jnp.zeros_like(inv_high)
    inv_low[...] = jnp.zeros_like(inv_low)
    for b in range(blocks):
        span = slice(b * rank, (b + 1) * rank)
        high, low = split(inv_small[b])
        inv_high[span, span] = high
        inv_low[span, span] = low
    size = rank
    while size < tile:
        for start in range(0, tile, 2 * size):
            first = slice(start, start + size)
            second = slice(start + size, start + 2 * size)
            middle = dot_split(split(diag_v[second, first]), (inv_high[first, first], inv_low[first, first]))
            cross = dot_split((inv_high[second, second], inv_low[second, second]), split(middle))
            high, low = split(-cross)
            inv_high[second, first] = high
            inv_low[second, first] = low
        size *= 2

    each(n_row, lambda d: rs_copy(d).wait_recv())
    mine = y_own[part(r)] - y_part[part(r)]
    for d in range(1, n_row):
        mine = mine - y_in[d - 1]
    y_full[part(r)] = mine
    each(n_row, lambda d: ag_copy(d, r).start())

    def pass_forward(d, e):
        pf_copy(d, e, chip_source(e)).wait_recv()
        sf_copy(d, e, chip_source(e)).start()

    each(n_row, lambda d: each(n_chip, lambda e: pass_forward(d, e)))
    each(n_row, lambda d: ag_copy(d, row_source(d)).wait_recv())

    sketched = y_full[...]
    sketched_ref[...] = sketched
    sketched_split = split(sketched)

    def across(left):
        return dot(left, sketched_split[0], TN) + dot(left, sketched_split[1], TN)

    inner = jnp.concatenate([across(slot_ref[0, 0, s, :, :rank]) for s in range(slots)], axis=0)
    x_all[r] = dot_wide(coupling[...], inner, TN)
    each(n_row, lambda d: x_copy(d, r).start())
    solved_ref[...] = dot_exact_left(a_right, across(a_left))

    gram = lax.dot_general(sketched, sketched, TN, precision=lax.Precision.HIGHEST, preferred_element_type=F32)
    state_gram, state_eye = gram, jnp.where(on_diag, 1.0, 0.0)
    group = 16
    sub_group = lax.broadcasted_iota(jnp.int32, (group, rank), 0)
    lane_group = lax.broadcasted_iota(jnp.int32, (group, rank), 1)
    for start in range(0, rank, group):
        block = state_gram[start:start + group]
        eye = state_eye[start:start + group]
        cols = [
            jnp.broadcast_to(block[:, start + u:start + u + 1], (group, rank)) for u in range(group)
        ]
        pivots = jnp.zeros((group, rank), F32)
        for t in range(group):
            pivot = cols[t][t:t + 1]
            pivots = jnp.where(sub_group == t, pivot, pivots)
            if t + 1 < group:
                factor = jnp.where(sub_group > t, cols[t] * (1.0 / pivot), 0.0)
                for u in range(t + 1, group):
                    cols[u] = cols[u] - factor * cols[u][t:t + 1]
                block = block - factor * block[t:t + 1]
                eye = eye - factor * eye[t:t + 1]
        scale = lax.rsqrt(pivots)
        block = block * scale
        eye = eye * scale
        hinv_ref[start:start + group] = eye
        if start + group < rank:
            left_high, left_low = split(jnp.where(lane_group >= start + group, block, 0.0))
            block_high, block_low = split(block)
            eye_high, eye_low = split(eye)
            left = jnp.concatenate([left_high, left_high, left_low, left_low], axis=0)
            state_gram = state_gram - dot(
                left, jnp.concatenate([block_high, block_low, block_high, block_low], axis=0), TN
            )
            state_eye = state_eye - dot(
                left, jnp.concatenate([eye_high, eye_low, eye_high, eye_low], axis=0), TN
            )

    projected = solved_ref[...]

    def take_forward(d):
        sf_copy(d, 0, sibling_source(0)).wait_recv()
        each(n_chip, lambda e: sf_copy(d, e, sibling_source(e)).wait_recv())

    each(n_row, take_forward)
    each(n_row, lambda d: x_copy(d, row_source(d)).wait_recv())
    for row in range(n_row):
        projected = projected - dot_exact_left(pu_all[row], x_all[row])
    solved_ref[...] = dot_split((inv_high[...], inv_low[...]), split(projected))

    def finish_chip(e):
        pv_copy(e, c).wait_send()
        pu_copy(e, c).wait_send()

    def finish_sibling(e):
        sv_copy(e, chip_source(e)).wait_send()
        su_copy(e, chip_source(e)).wait_send()

    def finish_row(d):
        pz_copy(d, r).wait_send()
        rs_copy(d).wait_send()
        ag_copy(d, r).wait_send()
        x_copy(d, r).wait_send()
        sf_copy(d, 0, c).wait_send()

    def finish_forward(d, e):
        pf_copy(d, e, c).wait_send()
        sf_copy(d, e, chip_source(e)).wait_send()

    each(n_chip, finish_chip)
    finish_sibling(0)
    each(n_chip, finish_sibling)
    each(n_row, finish_row)
    each(n_row, lambda d: each(n_chip, lambda e: finish_forward(d, e)))


def scale_kernel(sketched_ref, solved_ref, hinv_ref, basis_ref, coeff_ref):
    root = float(sketched_ref.shape[0]) ** 0.5
    factor = split(hinv_ref[...])
    basis_ref[0] = dot_split(split(sketched_ref[...]), factor, NT) * root
    coeff_ref[0] = dot_split(split(solved_ref[...]), factor, NT) * (1.0 / root)


def solution(mesh):
    n_row, n_col = mesh.shape["row"], mesh.shape["col"]

    def shards(slot_factors, slot_pairs, pivot_factors, a_factors, diag_factor, sketch):
        tile, rank = sketch.shape
        columns, rows = pivot_factors.shape[:2]
        slots = slot_factors.shape[2]
        chunk = tile // n_row
        vmem = pl.BlockSpec(memory_space=pltpu.VMEM)
        dma = pltpu.SemaphoreType.DMA
        out = jax.ShapeDtypeStruct((1, tile, rank), F32)
        n_chip = n_col // 2
        wide = jax.ShapeDtypeStruct((tile, rank), F32)
        sketched, solved, hinv = pl.pallas_call(
            functools.partial(kernel, n_row, n_col),
            out_shape=(wide, wide, jax.ShapeDtypeStruct((rank, rank), F32)),
            in_specs=[vmem, pl.BlockSpec(memory_space=pltpu.SMEM), vmem, vmem, pl.BlockSpec(memory_space=pl.ANY), vmem],
            out_specs=(vmem, vmem, vmem),
            scratch_shapes=[
                pltpu.VMEM((tile, tile), F32),
                pltpu.VMEM((tile // rank, rank, rank), F32),
                pltpu.VMEM((tile, tile), BF16),
                pltpu.VMEM((tile, tile), BF16),
                pltpu.VMEM((tile, columns * rank), BF16),
                pltpu.VMEM((n_row, tile, columns * rank), BF16),
                pltpu.VMEM((slots * rank, columns * rank), F32),
                pltpu.VMEM((tile, rank), F32),
                pltpu.VMEM((tile, rank), F32),
                pltpu.VMEM((n_row - 1, chunk, rank), F32),
                pltpu.VMEM((tile, rank), F32),
                pltpu.VMEM((n_row, columns * rank, rank), F32),
                dma(()),
                dma((n_chip - 1,)), dma((n_chip - 1,)),
                dma((n_chip - 1,)), dma((n_chip - 1,)),
                dma((n_chip,)), dma((n_chip,)),
                dma((n_chip,)), dma((n_chip,)),
                dma((n_row - 1,)), dma((n_row - 1,)),
                dma((n_row - 1, n_chip - 1)), dma((n_row - 1, n_chip - 1)),
                dma((n_row - 1, n_chip)), dma((n_row - 1, n_chip)),
                dma((n_row - 1,)), dma((n_row - 1,)),
                dma((n_row - 1,)), dma((n_row - 1,)),
                dma((n_row - 1,)), dma((n_row - 1,)),
            ],
            compiler_params=pltpu.CompilerParams(
                collective_id=0, has_side_effects=True, vmem_limit_bytes=56 * 1024 * 1024
            ),
            cost_estimate=pl.CostEstimate(flops=4 * 10**9, bytes_accessed=8 * 10**6, transcendentals=0),
        )(slot_factors, slot_pairs, pivot_factors, a_factors, diag_factor, sketch)
        return pl.pallas_call(
            scale_kernel,
            out_shape=(out, out),
            in_specs=[vmem, vmem, vmem],
            out_specs=(vmem, vmem),
            compiler_params=pltpu.CompilerParams(vmem_limit_bytes=24 * 1024 * 1024),
        )(sketched, solved, hinv)

    in_specs = (
        P("row", "col", None, None, None),
        P("row", "col", None),
        P("row", "col", None),
        P("col", None, None),
        P(),
        P(),
    )
    out_specs = (P("col", None, None), P("col", None, None))
    return jax.shard_map(shards, mesh=mesh, in_specs=in_specs, out_specs=out_specs, check_vma=False)
```

```python
import functools

import jax
import jax.numpy as jnp
from jax import lax
from jax.experimental import pallas as pl
from jax.experimental.pallas import tpu as pltpu
from jax.sharding import PartitionSpec as P

MESH = pl.DeviceIdType.MESH
F32 = jnp.float32
BF16 = jnp.bfloat16
NN = (((1,), (0,)), ((), ()))
TN = (((0,), (0,)), ((), ()))
NT = (((1,), (1,)), ((), ()))


def split(x):
    high = x.astype(BF16)
    return high, (x - high.astype(F32)).astype(BF16)


def dot(a, b, dims=NN):
    return lax.dot_general(a, b, dims, preferred_element_type=F32)


def dot_exact_left(a, b, dims=NN):
    high, low = split(b)
    return dot(a, high, dims) + dot(a, low, dims)


def dot_split(a, b, dims=NN):
    a_high, a_low = a
    b_high, b_low = b
    return dot(a_high, b_high, dims) + (dot(a_high, b_low, dims) + dot(a_low, b_high, dims))


def dot_wide(a, b, dims=NN):
    return dot_split(split(a), split(b), dims)


def kernel(
    n_row, n_col,
    slot_hbm, pairs_ref, pivot_ref, a_hbm, diag_ref, sketch_hbm,
    sketched_ref, solved_ref, hinv_ref,
    slot_ref, a_ref, sketch_ref, diag_v, inv_small, inv_high, inv_low, pv_all, pu_all, coupling,
    y_own, y_part, y_in, y_full, x_all, gram_v, inner_v,
    slot_sem, a_sem, sketch_sem, diag_sem, pv_send, pv_recv, pu_send, pu_recv, sv_send, sv_recv, su_send, su_recv, pz_send, pz_recv,
    pf_send, pf_recv, sf_send, sf_recv, rs_send, rs_recv, ag_send, ag_recv, x_send, x_recv,
):
    tile, rank = sketch_ref.shape
    columns, rows = pivot_ref.shape[0], pivot_ref.shape[1]
    slots = slot_ref.shape[2]
    chunk = tile // n_row
    r = lax.axis_index("row")
    c = lax.axis_index("col")
    n_chip = n_col // 2
    core, chip = lax.rem(c, 2), lax.div(c, 2)
    sibling = c + 1 - 2 * core

    a_copy = pltpu.make_async_copy(a_hbm, a_ref, a_sem)
    sketch_copy = pltpu.make_async_copy(sketch_hbm, sketch_ref, sketch_sem)
    slot_copy = pltpu.make_async_copy(slot_hbm, slot_ref, slot_sem)
    diag_copy = pltpu.make_async_copy(diag_ref, diag_v, diag_sem)
    a_copy.start()
    sketch_copy.start()
    diag_copy.start()
    slot_copy.start()

    def piece(index):
        return pl.ds(pl.multiple_of(index * rows, rows), rows)

    def part(index):
        return pl.ds(pl.multiple_of(index * chunk, chunk), chunk)

    for j in range(columns):
        lanes = slice(j * rank, (j + 1) * rank)
        pu_all[r, piece(c), lanes] = pivot_ref[j, :, :rank]
        pv_all[piece(c), lanes] = pivot_ref[j, :, rank:]

    barrier = pltpu.get_barrier_semaphore()

    def chip_mate(e):
        return lax.rem(chip + e, n_chip) * 2 + core

    def chip_source(e):
        return lax.rem(chip + n_chip - e, n_chip) * 2 + core

    def sibling_source(e):
        return lax.rem(chip + n_chip - e, n_chip) * 2 + 1 - core

    def greet_chip(e, _):
        pl.semaphore_signal(barrier, inc=1, device_id={"col": chip_mate(e)}, device_id_type=MESH)
        return 0

    def greet_row(d, _):
        pl.semaphore_signal(barrier, inc=1, device_id={"row": lax.rem(r + d, n_row)}, device_id_type=MESH)
        return 0

    lax.fori_loop(1, n_chip, greet_chip, 0)
    lax.fori_loop(1, n_row, greet_row, 0)
    pl.semaphore_signal(barrier, inc=1, device_id={"col": sibling}, device_id_type=MESH)
    pl.semaphore_wait(barrier, n_chip - 1 + n_row - 1 + 1)

    def to_col(ref, send, recv, target):
        return pltpu.make_async_remote_copy(
            ref, ref, send, recv, device_id={"col": target}, device_id_type=MESH
        )

    def to_row(source, target, send, recv, d):
        return pltpu.make_async_remote_copy(
            source, target, send, recv, device_id={"row": lax.rem(r + d, n_row)}, device_id_type=MESH
        )

    def pv_copy(e, index):
        return to_col(pv_all.at[piece(index)], pv_send.at[e - 1], pv_recv.at[e - 1], chip_mate(e))

    def pu_copy(e, index):
        return to_col(pu_all.at[r, piece(index)], pu_send.at[e - 1], pu_recv.at[e - 1], chip_mate(e))

    def sv_copy(e, index):
        return to_col(pv_all.at[piece(index)], sv_send.at[e], sv_recv.at[e], sibling)

    def su_copy(e, index):
        return to_col(pu_all.at[r, piece(index)], su_send.at[e], su_recv.at[e], sibling)

    def pz_copy(d, index):
        ref = pu_all.at[index, piece(c)]
        return to_row(ref, ref, pz_send.at[d - 1], pz_recv.at[d - 1], d)

    def pf_copy(d, e, index):
        ref = pu_all.at[row_source(d), piece(index)]
        return to_col(ref, pf_send.at[d - 1, e - 1], pf_recv.at[d - 1, e - 1], chip_mate(e))

    def sf_copy(d, e, index):
        ref = pu_all.at[row_source(d), piece(index)]
        return to_col(ref, sf_send.at[d - 1, e], sf_recv.at[d - 1, e], sibling)

    def rs_copy(d):
        return to_row(
            y_part.at[part(lax.rem(r + d, n_row))], y_in.at[d - 1], rs_send.at[d - 1], rs_recv.at[d - 1], d
        )

    def ag_copy(d, index):
        ref = y_full.at[part(index)]
        return to_row(ref, ref, ag_send.at[d - 1], ag_recv.at[d - 1], d)

    def x_copy(d, index):
        ref = x_all.at[index]
        return to_row(ref, ref, x_send.at[d - 1], x_recv.at[d - 1], d)

    def row_source(d):
        return lax.rem(r + n_row - d, n_row)

    def each(n, act):
        def body(d, _):
            act(d)
            return 0

        lax.fori_loop(1, n, body, 0)

    def push_pivots(e):
        pv_copy(e, c).start()
        pu_copy(e, c).start()

    each(n_chip, push_pivots)
    sv_copy(0, c).start()
    su_copy(0, c).start()
    each(n_row, lambda d: pz_copy(d, r).start())

    sketch_copy.wait()
    a_copy.wait()
    sketch_split = split(sketch_ref[...])
    a_left = a_ref[0, :, :rank]
    a_right = a_ref[0, :, rank:]
    a_sketch = dot(a_right, sketch_split[0], TN) + dot(a_right, sketch_split[1], TN)
    y_own[...] = dot_exact_left(a_left, a_sketch)

    def pass_pivots(e):
        pv_copy(e, chip_source(e)).wait_recv()
        sv_copy(e, chip_source(e)).start()
        pu_copy(e, chip_source(e)).wait_recv()
        su_copy(e, chip_source(e)).start()

    diag_copy.wait()
    blocks = tile // rank
    sub = lax.broadcasted_iota(jnp.int32, (rank, rank), 0)
    lane = lax.broadcasted_iota(jnp.int32, (rank, rank), 1)
    on_diag = sub == lane

    def diag_block(b):
        span = slice(b * rank, (b + 1) * rank)
        return diag_v[span, span]

    for b in range(blocks):
        low = diag_block(b)
        only = jnp.where(on_diag, low, 0.0)
        inv_sub = 1.0 / jnp.sum(only, axis=1, keepdims=True)
        inv_lane = 1.0 / jnp.sum(only, axis=0, keepdims=True)
        pair = (sub == lane + 1) & ((lane & 1) == 0)
        inv_small[b] = jnp.where(on_diag, inv_lane, 0.0) - jnp.where(pair, low * inv_sub * inv_lane, 0.0)

    def double(level, _):
        step = (lax.shift_right_logical(sub, level + 1) == lax.shift_right_logical(lane, level + 1)) & (
            lax.shift_right_logical(sub, level) != lax.shift_right_logical(lane, level)
        )
        for b in range(blocks):
            now = inv_small[b]
            now_split = split(now)
            cross = split(jnp.where(step, diag_block(b), 0.0))
            inv_small[b] = now - dot_split(split(dot_split(now_split, cross)), now_split)
        return 0

    levels = rank.bit_length() - 1
    early = 3
    lax.fori_loop(1, early, double, 0)
    each(n_chip, pass_pivots)
    slot_copy.wait()

    def take_pivots(e):
        sv_copy(e, sibling_source(e)).wait_recv()
        su_copy(e, sibling_source(e)).wait_recv()

    take_pivots(0)
    each(n_chip, take_pivots)
    pivot_right = pv_all[...]
    for s in range(slots):
        code = pairs_ref[0, 0, s]
        coupled = dot(slot_ref[0, 0, s, :, rank:], pivot_right, TN)
        for j in range(columns):
            lanes = slice(j * rank, (j + 1) * rank)
            coupling[s * rank:(s + 1) * rank, lanes] = jnp.where(code == j, coupled[:, lanes], 0.0)
    pivot_left = pu_all[r]
    weights = dot(pivot_left, sketch_split[0], TN) + dot(pivot_left, sketch_split[1], TN)
    mixed = dot_wide(coupling[...], weights)
    mixed_split = split(mixed)

    def update_rows(index):
        span = part(index)
        total = jnp.zeros((chunk, rank), F32)
        for s in range(slots):
            left = slot_ref[0, 0, s, span, :rank]
            for half in mixed_split:
                total += dot(left, half[s * rank:(s + 1) * rank])
        y_part[span] = total

    def push_update(d):
        update_rows(lax.rem(r + d, n_row))
        rs_copy(d).start()

    each(n_row, push_update)
    update_rows(r)

    def forward(d):
        pz_copy(d, row_source(d)).wait_recv()
        each(n_chip, lambda e: pf_copy(d, e, c).start())
        sf_copy(d, 0, c).start()

    each(n_row, forward)

    lax.fori_loop(early, levels, double, 0)

    each(n_row, lambda d: rs_copy(d).wait_recv())
    mine = y_own[part(r)] - y_part[part(r)]
    for d in range(1, n_row):
        mine = mine - y_in[d - 1]
    y_full[part(r)] = mine
    each(n_row, lambda d: ag_copy(d, r).start())

    def pass_forward(d, e):
        pf_copy(d, e, chip_source(e)).wait_recv()
        sf_copy(d, e, chip_source(e)).start()

    each(n_row, lambda d: each(n_chip, lambda e: pass_forward(d, e)))

    def products(index):
        span = part(index)
        piece_y = y_full[span]
        lefts = [slot_ref[0, 0, s, span, :rank] for s in range(slots)] + [a_ref[0, span, :rank]]
        inner = dot_exact_left(jnp.concatenate(lefts, axis=1), piece_y, TN)
        gram = lax.dot_general(
            piece_y, piece_y, TN, precision=lax.Precision.HIGHEST, preferred_element_type=F32
        )
        return inner, gram

    inner_v[...], gram_v[...] = products(r)

    inv_high[...] = jnp.zeros_like(inv_high)
    inv_low[...] = jnp.zeros_like(inv_low)
    for b in range(blocks):
        span = slice(b * rank, (b + 1) * rank)
        high, low = split(inv_small[b])
        inv_high[span, span] = high
        inv_low[span, span] = low
    size = rank
    while size < tile:
        for start in range(0, tile, 2 * size):
            first = slice(start, start + size)
            second = slice(start + size, start + 2 * size)
            middle = dot_split(split(diag_v[second, first]), (inv_high[first, first], inv_low[first, first]))
            cross = dot_split((inv_high[second, second], inv_low[second, second]), split(middle))
            high, low = split(-cross)
            inv_high[second, first] = high
            inv_low[second, first] = low
        size *= 2

    def take_chunk(d):
        ag_copy(d, row_source(d)).wait_recv()
        inner, gram = products(row_source(d))
        inner_v[...] += inner
        gram_v[...] += gram

    each(n_row, take_chunk)
    x_all[r] = dot_wide(coupling[...], inner_v[:slots * rank], TN)
    each(n_row, lambda d: x_copy(d, r).start())
    sketched_ref[...] = y_full[...]
    solved_ref[...] = dot_exact_left(a_right, inner_v[slots * rank:]) - dot_exact_left(pu_all[r], x_all[r])

    state_gram, state_eye = gram_v[...], jnp.where(on_diag, 1.0, 0.0)
    group = 16
    sub_group = lax.broadcasted_iota(jnp.int32, (group, rank), 0)
    lane_group = lax.broadcasted_iota(jnp.int32, (group, rank), 1)
    for start in range(0, rank, group):
        block = state_gram[start:start + group]
        eye = state_eye[start:start + group]
        cols = [
            jnp.broadcast_to(block[:, start + u:start + u + 1], (group, rank)) for u in range(group)
        ]
        pivots = jnp.zeros((group, rank), F32)
        for t in range(group):
            pivot = cols[t][t:t + 1]
            pivots = jnp.where(sub_group == t, pivot, pivots)
            if t + 1 < group:
                factor = jnp.where(sub_group > t, cols[t] * (1.0 / pivot), 0.0)
                for u in range(t + 1, group):
                    cols[u] = cols[u] - factor * cols[u][t:t + 1]
                block = block - factor * block[t:t + 1]
                eye = eye - factor * eye[t:t + 1]
        scale = lax.rsqrt(pivots)
        block = block * scale
        eye = eye * scale
        hinv_ref[start:start + group] = eye
        if start + group < rank:
            left_high, left_low = split(jnp.where(lane_group >= start + group, block, 0.0))
            block_high, block_low = split(block)
            eye_high, eye_low = split(eye)
            left = jnp.concatenate([left_high, left_high, left_low, left_low], axis=0)
            state_gram = state_gram - dot(
                left, jnp.concatenate([block_high, block_low, block_high, block_low], axis=0), TN
            )
            state_eye = state_eye - dot(
                left, jnp.concatenate([eye_high, eye_low, eye_high, eye_low], axis=0), TN
            )

    def take_product(d):
        sf_copy(d, 0, sibling_source(0)).wait_recv()
        each(n_chip, lambda e: sf_copy(d, e, sibling_source(e)).wait_recv())
        x_copy(d, row_source(d)).wait_recv()
        solved_ref[...] -= dot_exact_left(pu_all[row_source(d)], x_all[row_source(d)])

    each(n_row, take_product)
    high, low = split(solved_ref[...])
    band = 2 * rank
    for start in range(0, tile, band):
        span, upto = slice(start, start + band), slice(0, start + band)
        solved_ref[span] = dot_split((inv_high[span, upto], inv_low[span, upto]), (high[upto], low[upto]))

    def finish_chip(e):
        pv_copy(e, c).wait_send()
        pu_copy(e, c).wait_send()

    def finish_sibling(e):
        sv_copy(e, chip_source(e)).wait_send()
        su_copy(e, chip_source(e)).wait_send()

    def finish_row(d):
        pz_copy(d, r).wait_send()
        rs_copy(d).wait_send()
        ag_copy(d, r).wait_send()
        x_copy(d, r).wait_send()
        sf_copy(d, 0, c).wait_send()

    def finish_forward(d, e):
        pf_copy(d, e, c).wait_send()
        sf_copy(d, e, chip_source(e)).wait_send()

    each(n_chip, finish_chip)
    finish_sibling(0)
    each(n_chip, finish_sibling)
    each(n_row, finish_row)
    each(n_row, lambda d: each(n_chip, lambda e: finish_forward(d, e)))


def scale_kernel(sketched_ref, solved_ref, hinv_ref, basis_ref, coeff_ref):
    root = float(sketched_ref.shape[0]) ** 0.5
    factor = split(hinv_ref[...])
    basis_ref[0] = dot_split(split(sketched_ref[...]), factor, NT) * root
    coeff_ref[0] = dot_split(split(solved_ref[...]), factor, NT) * (1.0 / root)


def solution(mesh):
    n_row, n_col = mesh.shape["row"], mesh.shape["col"]

    def shards(slot_factors, slot_pairs, pivot_factors, a_factors, diag_factor, sketch):
        tile, rank = sketch.shape
        columns, rows = pivot_factors.shape[:2]
        slots = slot_factors.shape[2]
        chunk = tile // n_row
        vmem = pl.BlockSpec(memory_space=pltpu.VMEM)
        hbm = pl.BlockSpec(memory_space=pl.ANY)
        dma = pltpu.SemaphoreType.DMA
        out = jax.ShapeDtypeStruct((1, tile, rank), F32)
        n_chip = n_col // 2
        wide = jax.ShapeDtypeStruct((tile, rank), F32)
        sketched, solved, hinv = pl.pallas_call(
            functools.partial(kernel, n_row, n_col),
            out_shape=(wide, wide, jax.ShapeDtypeStruct((rank, rank), F32)),
            in_specs=[hbm, pl.BlockSpec(memory_space=pltpu.SMEM), vmem, hbm, hbm, hbm],
            out_specs=(vmem, vmem, vmem),
            scratch_shapes=[
                pltpu.VMEM(slot_factors.shape, BF16),
                pltpu.VMEM(a_factors.shape, BF16),
                pltpu.VMEM((tile, rank), F32),
                pltpu.VMEM((tile, tile), F32),
                pltpu.VMEM((tile // rank, rank, rank), F32),
                pltpu.VMEM((tile, tile), BF16),
                pltpu.VMEM((tile, tile), BF16),
                pltpu.VMEM((tile, columns * rank), BF16),
                pltpu.VMEM((n_row, tile, columns * rank), BF16),
                pltpu.VMEM((slots * rank, columns * rank), F32),
                pltpu.VMEM((tile, rank), F32),
                pltpu.VMEM((tile, rank), F32),
                pltpu.VMEM((n_row - 1, chunk, rank), F32),
                pltpu.VMEM((tile, rank), F32),
                pltpu.VMEM((n_row, columns * rank, rank), F32),
                pltpu.VMEM((rank, rank), F32),
                pltpu.VMEM(((slots + 1) * rank, rank), F32),
                dma(()), dma(()), dma(()), dma(()),
                dma((n_chip - 1,)), dma((n_chip - 1,)),
                dma((n_chip - 1,)), dma((n_chip - 1,)),
                dma((n_chip,)), dma((n_chip,)),
                dma((n_chip,)), dma((n_chip,)),
                dma((n_row - 1,)), dma((n_row - 1,)),
                dma((n_row - 1, n_chip - 1)), dma((n_row - 1, n_chip - 1)),
                dma((n_row - 1, n_chip)), dma((n_row - 1, n_chip)),
                dma((n_row - 1,)), dma((n_row - 1,)),
                dma((n_row - 1,)), dma((n_row - 1,)),
                dma((n_row - 1,)), dma((n_row - 1,)),
            ],
            compiler_params=pltpu.CompilerParams(
                collective_id=0, has_side_effects=True, vmem_limit_bytes=60 * 1024 * 1024
            ),
            cost_estimate=pl.CostEstimate(flops=4 * 10**9, bytes_accessed=8 * 10**6, transcendentals=0),
        )(slot_factors, slot_pairs, pivot_factors, a_factors, diag_factor, sketch)
        return pl.pallas_call(
            scale_kernel,
            out_shape=(out, out),
            in_specs=[vmem, vmem, vmem],
            out_specs=(vmem, vmem),
            compiler_params=pltpu.CompilerParams(vmem_limit_bytes=60 * 1024 * 1024),
        )(sketched, solved, hinv)

    in_specs = (
        P("row", "col", None, None, None),
        P("row", "col", None),
        P("row", "col", None),
        P("col", None, None),
        P(),
        P(),
    )
    out_specs = (P("col", None, None), P("col", None, None))
    return jax.shard_map(shards, mesh=mesh, in_specs=in_specs, out_specs=out_specs, check_vma=False)
```

```python
import functools

import jax
import jax.numpy as jnp
from jax import lax
from jax.experimental import pallas as pl
from jax.experimental.pallas import tpu as pltpu
from jax.sharding import PartitionSpec as P

HALVES = 2
MESH = pl.DeviceIdType.MESH
F32 = jnp.float32
BF16 = jnp.bfloat16
NN = (((1,), (0,)), ((), ()))
TN = (((0,), (0,)), ((), ()))
NT = (((1,), (1,)), ((), ()))


def split(x):
    high = x.astype(BF16)
    return high, (x - high.astype(F32)).astype(BF16)


def dot(a, b, dims=NN):
    return lax.dot_general(a, b, dims, preferred_element_type=F32)


def dot_exact_left(a, b, dims=NN):
    high, low = split(b)
    return dot(a, high, dims) + dot(a, low, dims)


def dot_split(a, b, dims=NN):
    a_high, a_low = a
    b_high, b_low = b
    return dot(a_high, b_high, dims) + (dot(a_high, b_low, dims) + dot(a_low, b_high, dims))


def dot_wide(a, b, dims=NN):
    return dot_split(split(a), split(b), dims)


def kernel(
    n_row, n_col,
    slot_hbm, pairs_ref, pivot_ref, a_hbm, diag_ref, sketch_hbm,
    sketched_ref, solved_ref, hinv_ref,
    slot_ref, a_ref, sketch_ref, diag_v, inv_small, inv_high, inv_low, pv_all, pu_all, coupling,
    y_own, y_part, y_in, y_full, x_all, gram_v, inner_v,
    slot_sem, a_sem, sketch_sem, diag_sem, pv_send, pv_recv, pu_send, pu_recv, sv_send, sv_recv, su_send, su_recv, pz_send, pz_recv,
    pf_send, pf_recv, sf_send, sf_recv, rs_send, rs_recv, ag_send, ag_recv, x_send, x_recv,
):
    tile, rank = sketch_ref.shape
    columns, rows = pivot_ref.shape[0], pivot_ref.shape[1]
    slots = slot_ref.shape[2]
    chunk = tile // n_row
    half = chunk // HALVES
    r = lax.axis_index("row")
    c = lax.axis_index("col")
    n_chip = n_col // 2
    core, chip = lax.rem(c, 2), lax.div(c, 2)
    sibling = c + 1 - 2 * core

    a_copy = pltpu.make_async_copy(a_hbm, a_ref, a_sem)
    sketch_copy = pltpu.make_async_copy(sketch_hbm, sketch_ref, sketch_sem)
    slot_copy = pltpu.make_async_copy(slot_hbm, slot_ref, slot_sem)
    diag_copy = pltpu.make_async_copy(diag_ref, diag_v, diag_sem)
    a_copy.start()
    sketch_copy.start()
    diag_copy.start()
    slot_copy.start()

    def piece(index):
        return pl.ds(pl.multiple_of(index * rows, rows), rows)

    def part(index, h):
        return pl.ds(pl.multiple_of(index * chunk + h * half, half), half)

    for j in range(columns):
        lanes = slice(j * rank, (j + 1) * rank)
        pu_all[r, piece(c), lanes] = pivot_ref[j, :, :rank]
        pv_all[piece(c), lanes] = pivot_ref[j, :, rank:]

    barrier = pltpu.get_barrier_semaphore()

    def chip_mate(e):
        return lax.rem(chip + e, n_chip) * 2 + core

    def chip_source(e):
        return lax.rem(chip + n_chip - e, n_chip) * 2 + core

    def sibling_source(e):
        return lax.rem(chip + n_chip - e, n_chip) * 2 + 1 - core

    def greet_chip(e, _):
        pl.semaphore_signal(barrier, inc=1, device_id={"col": chip_mate(e)}, device_id_type=MESH)
        return 0

    def greet_row(d, _):
        pl.semaphore_signal(barrier, inc=1, device_id={"row": lax.rem(r + d, n_row)}, device_id_type=MESH)
        return 0

    lax.fori_loop(1, n_chip, greet_chip, 0)
    lax.fori_loop(1, n_row, greet_row, 0)
    pl.semaphore_signal(barrier, inc=1, device_id={"col": sibling}, device_id_type=MESH)
    pl.semaphore_wait(barrier, n_chip - 1 + n_row - 1 + 1)

    def to_col(ref, send, recv, target):
        return pltpu.make_async_remote_copy(
            ref, ref, send, recv, device_id={"col": target}, device_id_type=MESH
        )

    def to_row(source, target, send, recv, d):
        return pltpu.make_async_remote_copy(
            source, target, send, recv, device_id={"row": lax.rem(r + d, n_row)}, device_id_type=MESH
        )

    def pv_copy(e, index):
        return to_col(pv_all.at[piece(index)], pv_send.at[e - 1], pv_recv.at[e - 1], chip_mate(e))

    def pu_copy(e, index):
        return to_col(pu_all.at[r, piece(index)], pu_send.at[e - 1], pu_recv.at[e - 1], chip_mate(e))

    def sv_copy(e, index):
        return to_col(pv_all.at[piece(index)], sv_send.at[e], sv_recv.at[e], sibling)

    def su_copy(e, index):
        return to_col(pu_all.at[r, piece(index)], su_send.at[e], su_recv.at[e], sibling)

    def pz_copy(d, index):
        ref = pu_all.at[index, piece(c)]
        return to_row(ref, ref, pz_send.at[d - 1], pz_recv.at[d - 1], d)

    def pf_copy(d, e, index):
        ref = pu_all.at[row_source(d), piece(index)]
        return to_col(ref, pf_send.at[d - 1, e - 1], pf_recv.at[d - 1, e - 1], chip_mate(e))

    def sf_copy(d, e, index):
        ref = pu_all.at[row_source(d), piece(index)]
        return to_col(ref, sf_send.at[d - 1, e], sf_recv.at[d - 1, e], sibling)

    def rs_copy(d, h):
        return to_row(
            y_part.at[part(lax.rem(r + d, n_row), h)], y_in.at[d - 1, h],
            rs_send.at[d - 1, h], rs_recv.at[d - 1, h], d,
        )

    def ag_copy(d, index, h):
        ref = y_full.at[part(index, h)]
        return to_row(ref, ref, ag_send.at[d - 1, h], ag_recv.at[d - 1, h], d)

    def x_copy(d, index):
        ref = x_all.at[index]
        return to_row(ref, ref, x_send.at[d - 1], x_recv.at[d - 1], d)

    def row_source(d):
        return lax.rem(r + n_row - d, n_row)

    def each(n, act):
        def body(d, _):
            act(d)
            return 0

        lax.fori_loop(1, n, body, 0)

    def push_pivots(e):
        pv_copy(e, c).start()
        pu_copy(e, c).start()

    each(n_chip, push_pivots)
    sv_copy(0, c).start()
    su_copy(0, c).start()
    each(n_row, lambda d: pz_copy(d, r).start())

    sketch_copy.wait()
    a_copy.wait()
    sketch_split = split(sketch_ref[...])
    a_left = a_ref[0, :, :rank]
    a_right = a_ref[0, :, rank:]
    a_sketch = dot(a_right, sketch_split[0], TN) + dot(a_right, sketch_split[1], TN)
    y_own[...] = dot_exact_left(a_left, a_sketch)

    def pass_pivots(e):
        pv_copy(e, chip_source(e)).wait_recv()
        sv_copy(e, chip_source(e)).start()
        pu_copy(e, chip_source(e)).wait_recv()
        su_copy(e, chip_source(e)).start()

    diag_copy.wait()
    blocks = tile // rank
    sub = lax.broadcasted_iota(jnp.int32, (rank, rank), 0)
    lane = lax.broadcasted_iota(jnp.int32, (rank, rank), 1)
    on_diag = sub == lane

    def diag_block(b):
        span = slice(b * rank, (b + 1) * rank)
        return diag_v[span, span]

    for b in range(blocks):
        low = diag_block(b)
        only = jnp.where(on_diag, low, 0.0)
        inv_sub = 1.0 / jnp.sum(only, axis=1, keepdims=True)
        inv_lane = 1.0 / jnp.sum(only, axis=0, keepdims=True)
        pair = (sub == lane + 1) & ((lane & 1) == 0)
        inv_small[b] = jnp.where(on_diag, inv_lane, 0.0) - jnp.where(pair, low * inv_sub * inv_lane, 0.0)

    def double(level, _):
        step = (lax.shift_right_logical(sub, level + 1) == lax.shift_right_logical(lane, level + 1)) & (
            lax.shift_right_logical(sub, level) != lax.shift_right_logical(lane, level)
        )
        for b in range(blocks):
            now = inv_small[b]
            now_split = split(now)
            cross = split(jnp.where(step, diag_block(b), 0.0))
            inv_small[b] = now - dot_split(split(dot_split(now_split, cross)), now_split)
        return 0

    levels = rank.bit_length() - 1
    early = 3
    lax.fori_loop(1, early, double, 0)
    each(n_chip, pass_pivots)
    slot_copy.wait()

    def take_pivots(e):
        sv_copy(e, sibling_source(e)).wait_recv()
        su_copy(e, sibling_source(e)).wait_recv()

    take_pivots(0)
    each(n_chip, take_pivots)
    pivot_right = pv_all[...]
    for s in range(slots):
        code = pairs_ref[0, 0, s]
        coupled = dot(slot_ref[0, 0, s, :, rank:], pivot_right, TN)
        for j in range(columns):
            lanes = slice(j * rank, (j + 1) * rank)
            coupling[s * rank:(s + 1) * rank, lanes] = jnp.where(code == j, coupled[:, lanes], 0.0)
    pivot_left = pu_all[r]
    weights = dot(pivot_left, sketch_split[0], TN) + dot(pivot_left, sketch_split[1], TN)
    mixed = dot_wide(coupling[...], weights)
    mixed_split = split(mixed)

    def update_rows(index, h):
        span = part(index, h)
        total = jnp.zeros((half, rank), F32)
        for s in range(slots):
            left = slot_ref[0, 0, s, span, :rank]
            for term in mixed_split:
                total += dot(left, term[s * rank:(s + 1) * rank])
        y_part[span] = total

    def push_update(d, h):
        update_rows(lax.rem(r + d, n_row), h)
        rs_copy(d, h).start()

    for h in range(HALVES):
        each(n_row, lambda d: push_update(d, h))
    for h in range(HALVES):
        update_rows(r, h)

    def forward(d):
        pz_copy(d, row_source(d)).wait_recv()
        each(n_chip, lambda e: pf_copy(d, e, c).start())
        sf_copy(d, 0, c).start()

    each(n_row, forward)

    lax.fori_loop(early, levels, double, 0)

    for h in range(HALVES):
        each(n_row, lambda d: rs_copy(d, h).wait_recv())
        mine = y_own[part(r, h)] - y_part[part(r, h)]
        for d in range(1, n_row):
            mine = mine - y_in[d - 1, h]
        y_full[part(r, h)] = mine
        each(n_row, lambda d: ag_copy(d, r, h).start())

    def pass_forward(d, e):
        pf_copy(d, e, chip_source(e)).wait_recv()
        sf_copy(d, e, chip_source(e)).start()

    each(n_row, lambda d: each(n_chip, lambda e: pass_forward(d, e)))

    def products(index, h):
        span = part(index, h)
        piece_y = y_full[span]
        lefts = [slot_ref[0, 0, s, span, :rank] for s in range(slots)] + [a_ref[0, span, :rank]]
        inner = dot_exact_left(jnp.concatenate(lefts, axis=1), piece_y, TN)
        gram = lax.dot_general(
            piece_y, piece_y, TN, precision=lax.Precision.HIGHEST, preferred_element_type=F32
        )
        return inner, gram

    inner_v[...] = jnp.zeros_like(inner_v)
    gram_v[...] = jnp.zeros_like(gram_v)

    def add_products(index, h):
        inner, gram = products(index, h)
        inner_v[...] += inner
        gram_v[...] += gram

    for h in range(HALVES):
        add_products(r, h)

    inv_high[...] = jnp.zeros_like(inv_high)
    inv_low[...] = jnp.zeros_like(inv_low)
    for b in range(blocks):
        span = slice(b * rank, (b + 1) * rank)
        high, low = split(inv_small[b])
        inv_high[span, span] = high
        inv_low[span, span] = low
    size = rank
    while size < tile:
        for start in range(0, tile, 2 * size):
            first = slice(start, start + size)
            second = slice(start + size, start + 2 * size)
            middle = dot_split(split(diag_v[second, first]), (inv_high[first, first], inv_low[first, first]))
            cross = dot_split((inv_high[second, second], inv_low[second, second]), split(middle))
            high, low = split(-cross)
            inv_high[second, first] = high
            inv_low[second, first] = low
        size *= 2

    def take_chunk(d, h):
        ag_copy(d, row_source(d), h).wait_recv()
        add_products(row_source(d), h)

    for h in range(HALVES):
        each(n_row, lambda d: take_chunk(d, h))
    x_all[r] = dot_wide(coupling[...], inner_v[:slots * rank], TN)
    each(n_row, lambda d: x_copy(d, r).start())
    sketched_ref[...] = y_full[...]
    solved_ref[...] = dot_exact_left(a_right, inner_v[slots * rank:]) - dot_exact_left(pu_all[r], x_all[r])

    state_gram, state_eye = gram_v[...], jnp.where(on_diag, 1.0, 0.0)
    group = 16
    sub_group = lax.broadcasted_iota(jnp.int32, (group, rank), 0)
    lane_group = lax.broadcasted_iota(jnp.int32, (group, rank), 1)
    for start in range(0, rank, group):
        block = state_gram[start:start + group]
        eye = state_eye[start:start + group]
        cols = [
            jnp.broadcast_to(block[:, start + u:start + u + 1], (group, rank)) for u in range(group)
        ]
        pivots = jnp.zeros((group, rank), F32)
        for t in range(group):
            pivot = cols[t][t:t + 1]
            pivots = jnp.where(sub_group == t, pivot, pivots)
            if t + 1 < group:
                factor = jnp.where(sub_group > t, cols[t] * (1.0 / pivot), 0.0)
                for u in range(t + 1, group):
                    cols[u] = cols[u] - factor * cols[u][t:t + 1]
                block = block - factor * block[t:t + 1]
                eye = eye - factor * eye[t:t + 1]
        scale = lax.rsqrt(pivots)
        block = block * scale
        eye = eye * scale
        hinv_ref[start:start + group] = eye
        if start + group < rank:
            left_high, left_low = split(jnp.where(lane_group >= start + group, block, 0.0))
            block_high, block_low = split(block)
            eye_high, eye_low = split(eye)
            left = jnp.concatenate([left_high, left_high, left_low, left_low], axis=0)
            state_gram = state_gram - dot(
                left, jnp.concatenate([block_high, block_low, block_high, block_low], axis=0), TN
            )
            state_eye = state_eye - dot(
                left, jnp.concatenate([eye_high, eye_low, eye_high, eye_low], axis=0), TN
            )

    def take_product(d):
        sf_copy(d, 0, sibling_source(0)).wait_recv()
        each(n_chip, lambda e: sf_copy(d, e, sibling_source(e)).wait_recv())
        x_copy(d, row_source(d)).wait_recv()
        solved_ref[...] -= dot_exact_left(pu_all[row_source(d)], x_all[row_source(d)])

    each(n_row, take_product)
    high, low = split(solved_ref[...])
    band = 2 * rank
    for start in range(0, tile, band):
        span, upto = slice(start, start + band), slice(0, start + band)
        solved_ref[span] = dot_split((inv_high[span, upto], inv_low[span, upto]), (high[upto], low[upto]))

    def finish_chip(e):
        pv_copy(e, c).wait_send()
        pu_copy(e, c).wait_send()

    def finish_sibling(e):
        sv_copy(e, chip_source(e)).wait_send()
        su_copy(e, chip_source(e)).wait_send()

    def finish_row(d):
        pz_copy(d, r).wait_send()
        for h in range(HALVES):
            rs_copy(d, h).wait_send()
            ag_copy(d, r, h).wait_send()
        x_copy(d, r).wait_send()
        sf_copy(d, 0, c).wait_send()

    def finish_forward(d, e):
        pf_copy(d, e, c).wait_send()
        sf_copy(d, e, chip_source(e)).wait_send()

    each(n_chip, finish_chip)
    finish_sibling(0)
    each(n_chip, finish_sibling)
    each(n_row, finish_row)
    each(n_row, lambda d: each(n_chip, lambda e: finish_forward(d, e)))


def scale_kernel(root, sketched_ref, solved_ref, hinv_ref, basis_ref, coeff_ref):
    factor = split(hinv_ref[...])
    basis_ref[0] = dot_split(split(sketched_ref[...]), factor, NT) * root
    coeff_ref[0] = dot_split(split(solved_ref[...]), factor, NT) * (1.0 / root)


def solution(mesh):
    n_row, n_col = mesh.shape["row"], mesh.shape["col"]

    def shards(slot_factors, slot_pairs, pivot_factors, a_factors, diag_factor, sketch):
        tile, rank = sketch.shape
        columns, rows = pivot_factors.shape[:2]
        slots = slot_factors.shape[2]
        chunk = tile // n_row
        vmem = pl.BlockSpec(memory_space=pltpu.VMEM)
        hbm = pl.BlockSpec(memory_space=pl.ANY)
        dma = pltpu.SemaphoreType.DMA
        out = jax.ShapeDtypeStruct((1, tile, rank), F32)
        n_chip = n_col // 2
        wide = jax.ShapeDtypeStruct((tile, rank), F32)
        sketched, solved, hinv = pl.pallas_call(
            functools.partial(kernel, n_row, n_col),
            out_shape=(wide, wide, jax.ShapeDtypeStruct((rank, rank), F32)),
            in_specs=[hbm, pl.BlockSpec(memory_space=pltpu.SMEM), vmem, hbm, hbm, hbm],
            out_specs=(vmem, vmem, vmem),
            scratch_shapes=[
                pltpu.VMEM(slot_factors.shape, BF16),
                pltpu.VMEM(a_factors.shape, BF16),
                pltpu.VMEM((tile, rank), F32),
                pltpu.VMEM((tile, tile), F32),
                pltpu.VMEM((tile // rank, rank, rank), F32),
                pltpu.VMEM((tile, tile), BF16),
                pltpu.VMEM((tile, tile), BF16),
                pltpu.VMEM((tile, columns * rank), BF16),
                pltpu.VMEM((n_row, tile, columns * rank), BF16),
                pltpu.VMEM((slots * rank, columns * rank), F32),
                pltpu.VMEM((tile, rank), F32),
                pltpu.VMEM((tile, rank), F32),
                pltpu.VMEM((n_row - 1, HALVES, chunk // HALVES, rank), F32),
                pltpu.VMEM((tile, rank), F32),
                pltpu.VMEM((n_row, columns * rank, rank), F32),
                pltpu.VMEM((rank, rank), F32),
                pltpu.VMEM(((slots + 1) * rank, rank), F32),
                dma(()), dma(()), dma(()), dma(()),
                dma((n_chip - 1,)), dma((n_chip - 1,)),
                dma((n_chip - 1,)), dma((n_chip - 1,)),
                dma((n_chip,)), dma((n_chip,)),
                dma((n_chip,)), dma((n_chip,)),
                dma((n_row - 1,)), dma((n_row - 1,)),
                dma((n_row - 1, n_chip - 1)), dma((n_row - 1, n_chip - 1)),
                dma((n_row - 1, n_chip)), dma((n_row - 1, n_chip)),
                dma((n_row - 1, HALVES)), dma((n_row - 1, HALVES)),
                dma((n_row - 1, HALVES)), dma((n_row - 1, HALVES)),
                dma((n_row - 1,)), dma((n_row - 1,)),
            ],
            compiler_params=pltpu.CompilerParams(
                collective_id=0, has_side_effects=True, vmem_limit_bytes=60 * 1024 * 1024
            ),
            cost_estimate=pl.CostEstimate(flops=4 * 10**9, bytes_accessed=8 * 10**6, transcendentals=0),
        )(slot_factors, slot_pairs, pivot_factors, a_factors, diag_factor, sketch)
        return pl.pallas_call(
            functools.partial(scale_kernel, float(tile) ** 0.5),
            out_shape=(out, out),
            grid=(4,),
            in_specs=[
                pl.BlockSpec((tile // 4, rank), lambda i: (i, 0)),
                pl.BlockSpec((tile // 4, rank), lambda i: (i, 0)),
                pl.BlockSpec((rank, rank), lambda i: (0, 0)),
            ],
            out_specs=(
                pl.BlockSpec((1, tile // 4, rank), lambda i: (0, i, 0)),
                pl.BlockSpec((1, tile // 4, rank), lambda i: (0, i, 0)),
            ),
            compiler_params=pltpu.CompilerParams(vmem_limit_bytes=60 * 1024 * 1024),
        )(sketched, solved, hinv)

    in_specs = (
        P("row", "col", None, None, None),
        P("row", "col", None),
        P("row", "col", None),
        P("col", None, None),
        P(),
        P(),
    )
    out_specs = (P("col", None, None), P("col", None, None))
    return jax.shard_map(shards, mesh=mesh, in_specs=in_specs, out_specs=out_specs, check_vma=False)
```

```python
import functools

import jax
import jax.numpy as jnp
from jax import lax
from jax.experimental import pallas as pl
from jax.experimental.pallas import tpu as pltpu
from jax.sharding import PartitionSpec as P

HALVES = 2
MESH = pl.DeviceIdType.MESH
F32 = jnp.float32
BF16 = jnp.bfloat16
NN = (((1,), (0,)), ((), ()))
TN = (((0,), (0,)), ((), ()))
NT = (((1,), (1,)), ((), ()))


def split(x):
    high = x.astype(BF16)
    return high, (x - high.astype(F32)).astype(BF16)


def dot(a, b, dims=NN):
    return lax.dot_general(a, b, dims, preferred_element_type=F32)


def fold(x):
    width = x.shape[1] // 2
    return x[:, :width] + x[:, width:]


def dot_exact_left(a, b, dims=NN):
    return fold(dot(a, jnp.concatenate(split(b), axis=1), dims))


def dot_split(a, b, dims=NN):
    a_high, a_low = a
    b_high, b_low = b
    if dims == NT or b_high.shape[1] > 128:
        return dot(a_high, b_high, dims) + (dot(a_high, b_low, dims) + dot(a_low, b_high, dims))
    both = jnp.concatenate([b_high, b_low], axis=1)
    if dims == NN and b_high.shape[0] <= 128:
        return fold(dot(jnp.concatenate([a_high, a_low], axis=1), jnp.concatenate([both, both], axis=0)))
    return fold(dot(a_high, both, dims)) + dot(a_low, b_high, dims)


def dot_wide(a, b, dims=NN):
    return dot_split(split(a), split(b), dims)


def kernel(
    n_row, n_col,
    slot_hbm, pairs_ref, pivot_ref, a_hbm, diag_ref, sketch_hbm,
    sketched_ref, solved_ref, hinv_ref,
    slot_ref, a_ref, sketch_ref, diag_v, inv_small, inv_high, inv_low, pv_all, pu_all, coupling,
    y_own, y_part, y_in, y_full, x_all, gram_v, inner_v,
    slot_sem, a_sem, sketch_sem, diag_sem, pv_send, pv_recv, pu_send, pu_recv, sv_send, sv_recv, su_send, su_recv, pz_send, pz_recv,
    pf_send, pf_recv, sf_send, sf_recv, rs_send, rs_recv, ag_send, ag_recv, x_send, x_recv,
):
    tile, rank = sketch_ref.shape
    columns, rows = pivot_ref.shape[0], pivot_ref.shape[1]
    slots = slot_ref.shape[2]
    chunk = tile // n_row
    half = chunk // HALVES
    r = lax.axis_index("row")
    c = lax.axis_index("col")
    n_chip = n_col // 2
    core, chip = lax.rem(c, 2), lax.div(c, 2)
    sibling = c + 1 - 2 * core

    a_copy = pltpu.make_async_copy(a_hbm, a_ref, a_sem)
    sketch_copy = pltpu.make_async_copy(sketch_hbm, sketch_ref, sketch_sem)
    slot_copy = pltpu.make_async_copy(slot_hbm, slot_ref, slot_sem)
    diag_copy = pltpu.make_async_copy(diag_ref, diag_v, diag_sem)
    a_copy.start()
    sketch_copy.start()
    diag_copy.start()
    slot_copy.start()

    def piece(index):
        return pl.ds(pl.multiple_of(index * rows, rows), rows)

    def part(index, h):
        return pl.ds(pl.multiple_of(index * chunk + h * half, half), half)

    for j in range(columns):
        lanes = slice(j * rank, (j + 1) * rank)
        pu_all[r, piece(c), lanes] = pivot_ref[j, :, :rank]
        pv_all[piece(c), lanes] = pivot_ref[j, :, rank:]

    barrier = pltpu.get_barrier_semaphore()

    def chip_mate(e):
        return lax.rem(chip + e, n_chip) * 2 + core

    def chip_source(e):
        return lax.rem(chip + n_chip - e, n_chip) * 2 + core

    def sibling_source(e):
        return lax.rem(chip + n_chip - e, n_chip) * 2 + 1 - core

    def greet_chip(e, _):
        pl.semaphore_signal(barrier, inc=1, device_id={"col": chip_mate(e)}, device_id_type=MESH)
        return 0

    def greet_row(d, _):
        pl.semaphore_signal(barrier, inc=1, device_id={"row": lax.rem(r + d, n_row)}, device_id_type=MESH)
        return 0

    lax.fori_loop(1, n_chip, greet_chip, 0)
    lax.fori_loop(1, n_row, greet_row, 0)
    pl.semaphore_signal(barrier, inc=1, device_id={"col": sibling}, device_id_type=MESH)
    pl.semaphore_wait(barrier, n_chip - 1 + n_row - 1 + 1)

    def to_col(ref, send, recv, target):
        return pltpu.make_async_remote_copy(
            ref, ref, send, recv, device_id={"col": target}, device_id_type=MESH
        )

    def to_row(source, target, send, recv, d):
        return pltpu.make_async_remote_copy(
            source, target, send, recv, device_id={"row": lax.rem(r + d, n_row)}, device_id_type=MESH
        )

    def pv_copy(e, index):
        return to_col(pv_all.at[piece(index)], pv_send.at[e - 1], pv_recv.at[e - 1], chip_mate(e))

    def pu_copy(e, index):
        return to_col(pu_all.at[r, piece(index)], pu_send.at[e - 1], pu_recv.at[e - 1], chip_mate(e))

    def sv_copy(e, index):
        return to_col(pv_all.at[piece(index)], sv_send.at[e], sv_recv.at[e], sibling)

    def su_copy(e, index):
        return to_col(pu_all.at[r, piece(index)], su_send.at[e], su_recv.at[e], sibling)

    def pz_copy(d, index):
        ref = pu_all.at[index, piece(c)]
        return to_row(ref, ref, pz_send.at[d - 1], pz_recv.at[d - 1], d)

    def pf_copy(d, e, index):
        ref = pu_all.at[row_source(d), piece(index)]
        return to_col(ref, pf_send.at[d - 1, e - 1], pf_recv.at[d - 1, e - 1], chip_mate(e))

    def sf_copy(d, e, index):
        ref = pu_all.at[row_source(d), piece(index)]
        return to_col(ref, sf_send.at[d - 1, e], sf_recv.at[d - 1, e], sibling)

    def rs_copy(d, h):
        return to_row(
            y_part.at[part(lax.rem(r + d, n_row), h)], y_in.at[d - 1, h],
            rs_send.at[d - 1, h], rs_recv.at[d - 1, h], d,
        )

    def ag_copy(d, index, h):
        ref = y_full.at[part(index, h)]
        return to_row(ref, ref, ag_send.at[d - 1, h], ag_recv.at[d - 1, h], d)

    def x_copy(d, index):
        ref = x_all.at[index]
        return to_row(ref, ref, x_send.at[d - 1], x_recv.at[d - 1], d)

    def row_source(d):
        return lax.rem(r + n_row - d, n_row)

    def each(n, act):
        def body(d, _):
            act(d)
            return 0

        lax.fori_loop(1, n, body, 0)

    def push_pivots(e):
        pv_copy(e, c).start()
        pu_copy(e, c).start()

    each(n_chip, push_pivots)
    sv_copy(0, c).start()
    su_copy(0, c).start()
    each(n_row, lambda d: pz_copy(d, r).start())

    sketch_copy.wait()
    a_copy.wait()
    sketch_split = split(sketch_ref[...])
    a_left = a_ref[0, :, :rank]
    a_right = a_ref[0, :, rank:]
    a_sketch = dot(a_right, sketch_split[0], TN) + dot(a_right, sketch_split[1], TN)
    y_own[...] = dot_exact_left(a_left, a_sketch)

    def pass_pivots(e):
        pv_copy(e, chip_source(e)).wait_recv()
        sv_copy(e, chip_source(e)).start()
        pu_copy(e, chip_source(e)).wait_recv()
        su_copy(e, chip_source(e)).start()

    diag_copy.wait()
    blocks = tile // rank
    sub = lax.broadcasted_iota(jnp.int32, (rank, rank), 0)
    lane = lax.broadcasted_iota(jnp.int32, (rank, rank), 1)
    on_diag = sub == lane

    def diag_block(b):
        span = slice(b * rank, (b + 1) * rank)
        return diag_v[span, span]

    for b in range(blocks):
        low = diag_block(b)
        only = jnp.where(on_diag, low, 0.0)
        inv_sub = 1.0 / jnp.sum(only, axis=1, keepdims=True)
        inv_lane = 1.0 / jnp.sum(only, axis=0, keepdims=True)
        pair = (sub == lane + 1) & ((lane & 1) == 0)
        inv_small[b] = jnp.where(on_diag, inv_lane, 0.0) - jnp.where(pair, low * inv_sub * inv_lane, 0.0)

    def double(level, _):
        step = (lax.shift_right_logical(sub, level + 1) == lax.shift_right_logical(lane, level + 1)) & (
            lax.shift_right_logical(sub, level) != lax.shift_right_logical(lane, level)
        )
        for b in range(blocks):
            now = inv_small[b]
            now_split = split(now)
            cross = split(jnp.where(step, diag_block(b), 0.0))
            inv_small[b] = now - dot_split(split(dot_split(now_split, cross)), now_split)
        return 0

    levels = rank.bit_length() - 1
    early = 3
    lax.fori_loop(1, early, double, 0)
    each(n_chip, pass_pivots)
    slot_copy.wait()

    def take_pivots(e):
        sv_copy(e, sibling_source(e)).wait_recv()
        su_copy(e, sibling_source(e)).wait_recv()

    take_pivots(0)
    each(n_chip, take_pivots)
    pivot_right = pv_all[...]
    for s in range(slots):
        code = pairs_ref[0, 0, s]
        coupled = dot(slot_ref[0, 0, s, :, rank:], pivot_right, TN)
        for j in range(columns):
            lanes = slice(j * rank, (j + 1) * rank)
            coupling[s * rank:(s + 1) * rank, lanes] = jnp.where(code == j, coupled[:, lanes], 0.0)
    pivot_left = pu_all[r]
    weights = dot(pivot_left, sketch_split[0], TN) + dot(pivot_left, sketch_split[1], TN)
    mixed = dot_wide(coupling[...], weights)
    mixed_split = split(mixed)

    def update_rows(index, h):
        span = part(index, h)
        total = jnp.zeros((half, rank), F32)
        for s in range(slots):
            left = slot_ref[0, 0, s, span, :rank]
            for term in mixed_split:
                total += dot(left, term[s * rank:(s + 1) * rank])
        y_part[span] = total

    def push_update(d, h):
        update_rows(lax.rem(r + d, n_row), h)
        rs_copy(d, h).start()

    for h in range(HALVES):
        each(n_row, lambda d: push_update(d, h))
    for h in range(HALVES):
        update_rows(r, h)

    def forward(d):
        pz_copy(d, row_source(d)).wait_recv()
        each(n_chip, lambda e: pf_copy(d, e, c).start())
        sf_copy(d, 0, c).start()

    each(n_row, forward)

    lax.fori_loop(early, levels, double, 0)

    for h in range(HALVES):
        each(n_row, lambda d: rs_copy(d, h).wait_recv())
        mine = y_own[part(r, h)] - y_part[part(r, h)]
        for d in range(1, n_row):
            mine = mine - y_in[d - 1, h]
        y_full[part(r, h)] = mine
        each(n_row, lambda d: ag_copy(d, r, h).start())

    def pass_forward(d, e):
        pf_copy(d, e, chip_source(e)).wait_recv()
        sf_copy(d, e, chip_source(e)).start()

    each(n_row, lambda d: each(n_chip, lambda e: pass_forward(d, e)))

    def products(index, h):
        span = part(index, h)
        halves = split(y_full[span])
        lefts = [slot_ref[0, 0, s, span, :rank] for s in range(slots)] + [a_ref[0, span, :rank]]
        whole = fold(dot(jnp.concatenate([*lefts, *halves], axis=1), jnp.concatenate(halves, axis=1), TN))
        edge = (slots + 1) * rank
        return whole[:edge], whole[edge:edge + rank] + whole[edge + rank:]

    inner_v[...] = jnp.zeros_like(inner_v)
    gram_v[...] = jnp.zeros_like(gram_v)

    def add_products(index, h):
        inner, gram = products(index, h)
        inner_v[...] += inner
        gram_v[...] += gram

    for h in range(HALVES):
        add_products(r, h)

    inv_high[...] = jnp.zeros_like(inv_high)
    inv_low[...] = jnp.zeros_like(inv_low)
    for b in range(blocks):
        span = slice(b * rank, (b + 1) * rank)
        high, low = split(inv_small[b])
        inv_high[span, span] = high
        inv_low[span, span] = low
    size = rank
    while size < tile:
        for start in range(0, tile, 2 * size):
            first = slice(start, start + size)
            second = slice(start + size, start + 2 * size)
            middle = dot_split(split(diag_v[second, first]), (inv_high[first, first], inv_low[first, first]))
            cross = dot_split((inv_high[second, second], inv_low[second, second]), split(middle))
            high, low = split(-cross)
            inv_high[second, first] = high
            inv_low[second, first] = low
        size *= 2

    def take_chunk(d, h):
        ag_copy(d, row_source(d), h).wait_recv()
        add_products(row_source(d), h)

    for h in range(HALVES):
        each(n_row, lambda d: take_chunk(d, h))
    x_all[r] = dot_wide(coupling[...], inner_v[:slots * rank], TN)
    each(n_row, lambda d: x_copy(d, r).start())
    sketched_ref[...] = y_full[...]
    solved_ref[...] = dot_exact_left(a_right, inner_v[slots * rank:]) - dot_exact_left(pu_all[r], x_all[r])

    state_gram, state_eye = gram_v[...], jnp.where(on_diag, 1.0, 0.0)
    group = 16
    sub_group = lax.broadcasted_iota(jnp.int32, (group, rank), 0)
    lane_group = lax.broadcasted_iota(jnp.int32, (group, rank), 1)
    for start in range(0, rank, group):
        block = state_gram[start:start + group]
        eye = state_eye[start:start + group]
        cols = [
            jnp.broadcast_to(block[:, start + u:start + u + 1], (group, rank)) for u in range(group)
        ]
        pivots = jnp.zeros((group, rank), F32)
        for t in range(group):
            pivot = cols[t][t:t + 1]
            pivots = jnp.where(sub_group == t, pivot, pivots)
            if t + 1 < group:
                factor = jnp.where(sub_group > t, cols[t] * (1.0 / pivot), 0.0)
                for u in range(t + 1, group):
                    cols[u] = cols[u] - factor * cols[u][t:t + 1]
                block = block - factor * block[t:t + 1]
                eye = eye - factor * eye[t:t + 1]
        scale = lax.rsqrt(pivots)
        block = block * scale
        eye = eye * scale
        hinv_ref[start:start + group] = eye
        if start + group < rank:
            left_high, left_low = split(jnp.where(lane_group >= start + group, block, 0.0))
            block_high, block_low = split(block)
            eye_high, eye_low = split(eye)
            left = jnp.concatenate([left_high, left_high, left_low, left_low], axis=0)
            state_gram = state_gram - dot(
                left, jnp.concatenate([block_high, block_low, block_high, block_low], axis=0), TN
            )
            state_eye = state_eye - dot(
                left, jnp.concatenate([eye_high, eye_low, eye_high, eye_low], axis=0), TN
            )

    def take_product(d):
        sf_copy(d, 0, sibling_source(0)).wait_recv()
        each(n_chip, lambda e: sf_copy(d, e, sibling_source(e)).wait_recv())
        x_copy(d, row_source(d)).wait_recv()
        solved_ref[...] -= dot_exact_left(pu_all[row_source(d)], x_all[row_source(d)])

    each(n_row, take_product)
    high, low = split(solved_ref[...])
    band = 2 * rank
    for start in range(0, tile, band):
        span, upto = slice(start, start + band), slice(0, start + band)
        solved_ref[span] = dot_split((inv_high[span, upto], inv_low[span, upto]), (high[upto], low[upto]))

    def finish_chip(e):
        pv_copy(e, c).wait_send()
        pu_copy(e, c).wait_send()

    def finish_sibling(e):
        sv_copy(e, chip_source(e)).wait_send()
        su_copy(e, chip_source(e)).wait_send()

    def finish_row(d):
        pz_copy(d, r).wait_send()
        for h in range(HALVES):
            rs_copy(d, h).wait_send()
            ag_copy(d, r, h).wait_send()
        x_copy(d, r).wait_send()
        sf_copy(d, 0, c).wait_send()

    def finish_forward(d, e):
        pf_copy(d, e, c).wait_send()
        sf_copy(d, e, chip_source(e)).wait_send()

    each(n_chip, finish_chip)
    finish_sibling(0)
    each(n_chip, finish_sibling)
    each(n_row, finish_row)
    each(n_row, lambda d: each(n_chip, lambda e: finish_forward(d, e)))


def scale_kernel(root, sketched_ref, solved_ref, hinv_ref, basis_ref, coeff_ref):
    factor = split(hinv_ref[...])
    basis_ref[0] = dot_split(split(sketched_ref[...]), factor, NT) * root
    coeff_ref[0] = dot_split(split(solved_ref[...]), factor, NT) * (1.0 / root)


def solution(mesh):
    n_row, n_col = mesh.shape["row"], mesh.shape["col"]

    def shards(slot_factors, slot_pairs, pivot_factors, a_factors, diag_factor, sketch):
        tile, rank = sketch.shape
        columns, rows = pivot_factors.shape[:2]
        slots = slot_factors.shape[2]
        chunk = tile // n_row
        vmem = pl.BlockSpec(memory_space=pltpu.VMEM)
        hbm = pl.BlockSpec(memory_space=pl.ANY)
        dma = pltpu.SemaphoreType.DMA
        out = jax.ShapeDtypeStruct((1, tile, rank), F32)
        n_chip = n_col // 2
        wide = jax.ShapeDtypeStruct((tile, rank), F32)
        sketched, solved, hinv = pl.pallas_call(
            functools.partial(kernel, n_row, n_col),
            out_shape=(wide, wide, jax.ShapeDtypeStruct((rank, rank), F32)),
            in_specs=[hbm, pl.BlockSpec(memory_space=pltpu.SMEM), vmem, hbm, hbm, hbm],
            out_specs=(vmem, vmem, vmem),
            scratch_shapes=[
                pltpu.VMEM(slot_factors.shape, BF16),
                pltpu.VMEM(a_factors.shape, BF16),
                pltpu.VMEM((tile, rank), F32),
                pltpu.VMEM((tile, tile), F32),
                pltpu.VMEM((tile // rank, rank, rank), F32),
                pltpu.VMEM((tile, tile), BF16),
                pltpu.VMEM((tile, tile), BF16),
                pltpu.VMEM((tile, columns * rank), BF16),
                pltpu.VMEM((n_row, tile, columns * rank), BF16),
                pltpu.VMEM((slots * rank, columns * rank), F32),
                pltpu.VMEM((tile, rank), F32),
                pltpu.VMEM((tile, rank), F32),
                pltpu.VMEM((n_row - 1, HALVES, chunk // HALVES, rank), F32),
                pltpu.VMEM((tile, rank), F32),
                pltpu.VMEM((n_row, columns * rank, rank), F32),
                pltpu.VMEM((rank, rank), F32),
                pltpu.VMEM(((slots + 1) * rank, rank), F32),
                dma(()), dma(()), dma(()), dma(()),
                dma((n_chip - 1,)), dma((n_chip - 1,)),
                dma((n_chip - 1,)), dma((n_chip - 1,)),
                dma((n_chip,)), dma((n_chip,)),
                dma((n_chip,)), dma((n_chip,)),
                dma((n_row - 1,)), dma((n_row - 1,)),
                dma((n_row - 1, n_chip - 1)), dma((n_row - 1, n_chip - 1)),
                dma((n_row - 1, n_chip)), dma((n_row - 1, n_chip)),
                dma((n_row - 1, HALVES)), dma((n_row - 1, HALVES)),
                dma((n_row - 1, HALVES)), dma((n_row - 1, HALVES)),
                dma((n_row - 1,)), dma((n_row - 1,)),
            ],
            compiler_params=pltpu.CompilerParams(
                collective_id=0, has_side_effects=True, vmem_limit_bytes=60 * 1024 * 1024
            ),
            cost_estimate=pl.CostEstimate(flops=4 * 10**9, bytes_accessed=8 * 10**6, transcendentals=0),
        )(slot_factors, slot_pairs, pivot_factors, a_factors, diag_factor, sketch)
        return pl.pallas_call(
            functools.partial(scale_kernel, float(tile) ** 0.5),
            out_shape=(out, out),
            in_specs=[vmem, vmem, vmem],
            out_specs=(vmem, vmem),
            compiler_params=pltpu.CompilerParams(vmem_limit_bytes=60 * 1024 * 1024),
        )(sketched, solved, hinv)

    in_specs = (
        P("row", "col", None, None, None),
        P("row", "col", None),
        P("row", "col", None),
        P("col", None, None),
        P(),
        P(),
    )
    out_specs = (P("col", None, None), P("col", None, None))
    return jax.shard_map(shards, mesh=mesh, in_specs=in_specs, out_specs=out_specs, check_vma=False)
```

```python
import functools

import jax
import jax.numpy as jnp
from jax import lax
from jax.experimental import pallas as pl
from jax.experimental.pallas import tpu as pltpu
from jax.sharding import PartitionSpec as P

HALVES = 2
MESH = pl.DeviceIdType.MESH
F32 = jnp.float32
BF16 = jnp.bfloat16
NN = (((1,), (0,)), ((), ()))
TN = (((0,), (0,)), ((), ()))
NT = (((1,), (1,)), ((), ()))


def split(x):
    high = x.astype(BF16)
    return high, (x - high.astype(F32)).astype(BF16)


def dot(a, b, dims=NN):
    return lax.dot_general(a, b, dims, preferred_element_type=F32)


def fold(x):
    width = x.shape[1] // 2
    return x[:, :width] + x[:, width:]


def dot_exact_left(a, b, dims=NN):
    return fold(dot(a, jnp.concatenate(split(b), axis=1), dims))


def dot_split(a, b, dims=NN):
    a_high, a_low = a
    b_high, b_low = b
    if dims == NT or b_high.shape[1] > 128:
        return dot(a_high, b_high, dims) + (dot(a_high, b_low, dims) + dot(a_low, b_high, dims))
    both = jnp.concatenate([b_high, b_low], axis=1)
    if dims == NN and b_high.shape[0] <= 128:
        return fold(dot(jnp.concatenate([a_high, a_low], axis=1), jnp.concatenate([both, both], axis=0)))
    return fold(dot(a_high, both, dims)) + dot(a_low, b_high, dims)


def dot_wide(a, b, dims=NN):
    return dot_split(split(a), split(b), dims)


def kernel(
    n_row, n_col,
    slot_hbm, pairs_ref, pivot_ref, a_hbm, diag_ref, sketch_hbm,
    sketched_ref, solved_ref, hinv_ref,
    slot_ref, a_ref, sketch_ref, diag_v, inv_small, inv_high, inv_low, pv_all, pu_all, coupling,
    y_own, y_part, y_in, y_full, x_all, gram_v, inner_v,
    slot_sem, a_sem, sketch_sem, diag_sem, pv_send, pv_recv, pu_send, pu_recv, sv_send, sv_recv, su_send, su_recv, pz_send, pz_recv,
    pf_send, pf_recv, sf_send, sf_recv, rs_send, rs_recv, ag_send, ag_recv, x_send, x_recv,
):
    tile, rank = sketch_ref.shape
    columns, rows = pivot_ref.shape[0], pivot_ref.shape[1]
    slots = slot_ref.shape[2]
    chunk = tile // n_row
    half = chunk // HALVES
    r = lax.axis_index("row")
    c = lax.axis_index("col")
    n_chip = n_col // 2
    core, chip = lax.rem(c, 2), lax.div(c, 2)
    sibling = c + 1 - 2 * core

    a_copy = pltpu.make_async_copy(a_hbm, a_ref, a_sem)
    sketch_copy = pltpu.make_async_copy(sketch_hbm, sketch_ref, sketch_sem)
    slot_copy = pltpu.make_async_copy(slot_hbm, slot_ref, slot_sem)
    diag_copy = pltpu.make_async_copy(diag_ref, diag_v, diag_sem)
    a_copy.start()
    sketch_copy.start()
    diag_copy.start()
    slot_copy.start()

    def piece(index):
        return pl.ds(pl.multiple_of(index * rows, rows), rows)

    def part(index, h):
        return pl.ds(pl.multiple_of(index * chunk + h * half, half), half)

    for j in range(columns):
        lanes = slice(j * rank, (j + 1) * rank)
        pu_all[r, piece(c), lanes] = pivot_ref[j, :, :rank]
        pv_all[piece(c), lanes] = pivot_ref[j, :, rank:]

    barrier = pltpu.get_barrier_semaphore()

    def chip_mate(e):
        return lax.rem(chip + e, n_chip) * 2 + core

    def chip_source(e):
        return lax.rem(chip + n_chip - e, n_chip) * 2 + core

    def sibling_source(e):
        return lax.rem(chip + n_chip - e, n_chip) * 2 + 1 - core

    def greet_chip(e, _):
        pl.semaphore_signal(barrier, inc=1, device_id={"col": chip_mate(e)}, device_id_type=MESH)
        return 0

    def greet_row(d, _):
        pl.semaphore_signal(barrier, inc=1, device_id={"row": lax.rem(r + d, n_row)}, device_id_type=MESH)
        return 0

    lax.fori_loop(1, n_chip, greet_chip, 0)
    lax.fori_loop(1, n_row, greet_row, 0)
    pl.semaphore_signal(barrier, inc=1, device_id={"col": sibling}, device_id_type=MESH)
    pl.semaphore_wait(barrier, n_chip - 1 + n_row - 1 + 1)

    def to_col(ref, send, recv, target):
        return pltpu.make_async_remote_copy(
            ref, ref, send, recv, device_id={"col": target}, device_id_type=MESH
        )

    def to_row(source, target, send, recv, d):
        return pltpu.make_async_remote_copy(
            source, target, send, recv, device_id={"row": lax.rem(r + d, n_row)}, device_id_type=MESH
        )

    def pv_copy(e, index):
        return to_col(pv_all.at[piece(index)], pv_send.at[e - 1], pv_recv.at[e - 1], chip_mate(e))

    def pu_copy(e, index):
        return to_col(pu_all.at[r, piece(index)], pu_send.at[e - 1], pu_recv.at[e - 1], chip_mate(e))

    def sv_copy(e, index):
        return to_col(pv_all.at[piece(index)], sv_send.at[e], sv_recv.at[e], sibling)

    def su_copy(e, index):
        return to_col(pu_all.at[r, piece(index)], su_send.at[e], su_recv.at[e], sibling)

    def pz_copy(d, index):
        ref = pu_all.at[index, piece(c)]
        return to_row(ref, ref, pz_send.at[d - 1], pz_recv.at[d - 1], d)

    def pf_copy(d, e, index):
        ref = pu_all.at[row_source(d), piece(index)]
        return to_col(ref, pf_send.at[d - 1, e - 1], pf_recv.at[d - 1, e - 1], chip_mate(e))

    def sf_copy(d, e, index):
        ref = pu_all.at[row_source(d), piece(index)]
        return to_col(ref, sf_send.at[d - 1, e], sf_recv.at[d - 1, e], sibling)

    def rs_copy(d, h):
        return to_row(
            y_part.at[part(lax.rem(r + d, n_row), h)], y_in.at[d - 1, h],
            rs_send.at[d - 1, h], rs_recv.at[d - 1, h], d,
        )

    def ag_copy(d, index, h):
        ref = y_full.at[part(index, h)]
        return to_row(ref, ref, ag_send.at[d - 1, h], ag_recv.at[d - 1, h], d)

    def x_copy(d, index):
        ref = x_all.at[index]
        return to_row(ref, ref, x_send.at[d - 1], x_recv.at[d - 1], d)

    def row_source(d):
        return lax.rem(r + n_row - d, n_row)

    def each(n, act):
        def body(d, _):
            act(d)
            return 0

        lax.fori_loop(1, n, body, 0)

    def push_pivots(e):
        pv_copy(e, c).start()
        pu_copy(e, c).start()

    each(n_chip, push_pivots)
    sv_copy(0, c).start()
    su_copy(0, c).start()
    each(n_row, lambda d: pz_copy(d, r).start())

    sketch_copy.wait()
    a_copy.wait()
    sketch_split = split(sketch_ref[...])
    a_left = a_ref[0, :, :rank]
    a_right = a_ref[0, :, rank:]
    a_sketch = dot(a_right, sketch_split[0], TN) + dot(a_right, sketch_split[1], TN)
    y_own[...] = dot_exact_left(a_left, a_sketch)

    def pass_pivots(e):
        pv_copy(e, chip_source(e)).wait_recv()
        sv_copy(e, chip_source(e)).start()
        pu_copy(e, chip_source(e)).wait_recv()
        su_copy(e, chip_source(e)).start()

    diag_copy.wait()
    blocks = tile // rank
    sub = lax.broadcasted_iota(jnp.int32, (rank, rank), 0)
    lane = lax.broadcasted_iota(jnp.int32, (rank, rank), 1)
    on_diag = sub == lane

    def diag_block(b):
        span = slice(b * rank, (b + 1) * rank)
        return diag_v[span, span]

    for b in range(blocks):
        low = diag_block(b)
        only = jnp.where(on_diag, low, 0.0)
        inv_sub = 1.0 / jnp.sum(only, axis=1, keepdims=True)
        inv_lane = 1.0 / jnp.sum(only, axis=0, keepdims=True)
        pair = (sub == lane + 1) & ((lane & 1) == 0)
        inv_small[b] = jnp.where(on_diag, inv_lane, 0.0) - jnp.where(pair, low * inv_sub * inv_lane, 0.0)

    def double(level, _):
        step = (lax.shift_right_logical(sub, level + 1) == lax.shift_right_logical(lane, level + 1)) & (
            lax.shift_right_logical(sub, level) != lax.shift_right_logical(lane, level)
        )
        for b in range(blocks):
            now = inv_small[b]
            now_split = split(now)
            cross = split(jnp.where(step, diag_block(b), 0.0))
            inv_small[b] = now - dot_split(split(dot_split(now_split, cross)), now_split)
        return 0

    levels = rank.bit_length() - 1
    early = 3
    lax.fori_loop(1, early, double, 0)
    each(n_chip, pass_pivots)
    slot_copy.wait()

    def take_pivots(e):
        sv_copy(e, sibling_source(e)).wait_recv()
        su_copy(e, sibling_source(e)).wait_recv()

    take_pivots(0)
    each(n_chip, take_pivots)
    pivot_right = pv_all[...]
    for s in range(slots):
        code = pairs_ref[0, 0, s]
        coupled = dot(slot_ref[0, 0, s, :, rank:], pivot_right, TN)
        for j in range(columns):
            lanes = slice(j * rank, (j + 1) * rank)
            coupling[s * rank:(s + 1) * rank, lanes] = jnp.where(code == j, coupled[:, lanes], 0.0)
    pivot_left = pu_all[r]
    weights = dot(pivot_left, sketch_split[0], TN) + dot(pivot_left, sketch_split[1], TN)
    mixed = dot_wide(coupling[...], weights)
    mixed_split = split(mixed)

    def update_rows(index, h):
        span = part(index, h)
        total = jnp.zeros((half, rank), F32)
        for s in range(slots):
            left = slot_ref[0, 0, s, span, :rank]
            for term in mixed_split:
                total += dot(left, term[s * rank:(s + 1) * rank])
        y_part[span] = total

    def push_update(d, h):
        update_rows(lax.rem(r + d, n_row), h)
        rs_copy(d, h).start()

    for h in range(HALVES):
        each(n_row, lambda d: push_update(d, h))
    for h in range(HALVES):
        update_rows(r, h)

    def forward(d):
        pz_copy(d, row_source(d)).wait_recv()
        each(n_chip, lambda e: pf_copy(d, e, c).start())
        sf_copy(d, 0, c).start()

    each(n_row, forward)

    lax.fori_loop(early, levels, double, 0)

    for h in range(HALVES):
        each(n_row, lambda d: rs_copy(d, h).wait_recv())
        mine = y_own[part(r, h)] - y_part[part(r, h)]
        for d in range(1, n_row):
            mine = mine - y_in[d - 1, h]
        y_full[part(r, h)] = mine
        each(n_row, lambda d: ag_copy(d, r, h).start())

    def pass_forward(d, e):
        pf_copy(d, e, chip_source(e)).wait_recv()
        sf_copy(d, e, chip_source(e)).start()

    each(n_row, lambda d: each(n_chip, lambda e: pass_forward(d, e)))

    def products(index, h):
        span = part(index, h)
        halves = split(y_full[span])
        lefts = [slot_ref[0, 0, s, span, :rank] for s in range(slots)] + [a_ref[0, span, :rank]]
        whole = fold(dot(jnp.concatenate([*lefts, *halves], axis=1), jnp.concatenate(halves, axis=1), TN))
        edge = (slots + 1) * rank
        return whole[:edge], whole[edge:edge + rank] + whole[edge + rank:]

    inner_v[...] = jnp.zeros_like(inner_v)
    gram_v[...] = jnp.zeros_like(gram_v)

    def add_products(index, h):
        inner, gram = products(index, h)
        inner_v[...] += inner
        gram_v[...] += gram

    for h in range(HALVES):
        add_products(r, h)

    inv_high[...] = jnp.zeros_like(inv_high)
    inv_low[...] = jnp.zeros_like(inv_low)
    for b in range(blocks):
        span = slice(b * rank, (b + 1) * rank)
        high, low = split(inv_small[b])
        inv_high[span, span] = high
        inv_low[span, span] = low
    size = rank
    while size < tile:
        for start in range(0, tile, 2 * size):
            first = slice(start, start + size)
            second = slice(start + size, start + 2 * size)
            middle = dot_split(split(diag_v[second, first]), (inv_high[first, first], inv_low[first, first]))
            cross = dot_split((inv_high[second, second], inv_low[second, second]), split(middle))
            high, low = split(-cross)
            inv_high[second, first] = high
            inv_low[second, first] = low
        size *= 2

    def take_chunk(d, h):
        ag_copy(d, row_source(d), h).wait_recv()
        add_products(row_source(d), h)

    for h in range(HALVES):
        each(n_row, lambda d: take_chunk(d, h))
    x_all[r] = dot_wide(coupling[...], inner_v[:slots * rank], TN)
    each(n_row, lambda d: x_copy(d, r).start())
    sketched_ref[...] = y_full[...]
    solved_ref[...] = dot_exact_left(a_right, inner_v[slots * rank:]) - dot_exact_left(pu_all[r], x_all[r])

    state_gram, state_eye = gram_v[...], jnp.where(on_diag, 1.0, 0.0)
    group = 16
    sub_half = lax.broadcasted_iota(jnp.int32, (8, rank), 0)
    tops = range(0, group, 8)
    lane_group = lax.broadcasted_iota(jnp.int32, (group, rank), 1)
    for start in range(0, rank, group):
        block = [state_gram[start + p:start + p + 8] for p in tops]
        eye = [state_eye[start + p:start + p + 8] for p in tops]
        cols = [
            [jnp.broadcast_to(piece[:, start + u:start + u + 1], (8, rank)) for piece in block]
            for u in range(group)
        ]
        pivots = [jnp.ones((8, rank), F32) for _ in tops]
        for t in range(group):
            own, row = t // 8, slice(t % 8, t % 8 + 1)
            pivot = cols[t][own][row]
            pivots[own] = jnp.where(sub_half == t % 8, pivot, pivots[own])
            inverse = 1.0 / pivot
            heads = [cols[u][own][row] for u in range(t + 1, group)]
            head_block, head_eye = block[own][row], eye[own][row]
            for p in range(own, len(block)):
                if p == own and t % 8 == 7:
                    continue
                factor = cols[t][p] * inverse
                if p == own:
                    factor = jnp.where(sub_half > t % 8, factor, 0.0)
                for u in range(t + 1, group):
                    cols[u][p] = cols[u][p] - factor * heads[u - t - 1]
                block[p] = block[p] - factor * head_block
                eye[p] = eye[p] - factor * head_eye
        block = jnp.concatenate(block, axis=0)
        eye = jnp.concatenate(eye, axis=0)
        pivots = jnp.concatenate(pivots, axis=0)
        scale = lax.rsqrt(pivots)
        block = block * scale
        eye = eye * scale
        hinv_ref[start:start + group] = eye
        if start + group < rank:
            left_high, left_low = split(jnp.where(lane_group >= start + group, block, 0.0))
            block_high, block_low = split(block)
            eye_high, eye_low = split(eye)
            left = jnp.concatenate([left_high, left_high, left_low, left_low], axis=0)
            state_gram = state_gram - dot(
                left, jnp.concatenate([block_high, block_low, block_high, block_low], axis=0), TN
            )
            state_eye = state_eye - dot(
                left, jnp.concatenate([eye_high, eye_low, eye_high, eye_low], axis=0), TN
            )

    def take_product(d):
        sf_copy(d, 0, sibling_source(0)).wait_recv()
        each(n_chip, lambda e: sf_copy(d, e, sibling_source(e)).wait_recv())
        x_copy(d, row_source(d)).wait_recv()
        solved_ref[...] -= dot_exact_left(pu_all[row_source(d)], x_all[row_source(d)])

    each(n_row, take_product)
    high, low = split(solved_ref[...])
    band = 2 * rank
    for start in range(0, tile, band):
        span, upto = slice(start, start + band), slice(0, start + band)
        solved_ref[span] = dot_split((inv_high[span, upto], inv_low[span, upto]), (high[upto], low[upto]))

    def finish_chip(e):
        pv_copy(e, c).wait_send()
        pu_copy(e, c).wait_send()

    def finish_sibling(e):
        sv_copy(e, chip_source(e)).wait_send()
        su_copy(e, chip_source(e)).wait_send()

    def finish_row(d):
        pz_copy(d, r).wait_send()
        for h in range(HALVES):
            rs_copy(d, h).wait_send()
            ag_copy(d, r, h).wait_send()
        x_copy(d, r).wait_send()
        sf_copy(d, 0, c).wait_send()

    def finish_forward(d, e):
        pf_copy(d, e, c).wait_send()
        sf_copy(d, e, chip_source(e)).wait_send()

    each(n_chip, finish_chip)
    finish_sibling(0)
    each(n_chip, finish_sibling)
    each(n_row, finish_row)
    each(n_row, lambda d: each(n_chip, lambda e: finish_forward(d, e)))


def scale_kernel(root, sketched_ref, solved_ref, hinv_ref, basis_ref, coeff_ref):
    factor = split(hinv_ref[...])
    basis_ref[0] = dot_split(split(sketched_ref[...]), factor, NT) * root
    coeff_ref[0] = dot_split(split(solved_ref[...]), factor, NT) * (1.0 / root)


def solution(mesh):
    n_row, n_col = mesh.shape["row"], mesh.shape["col"]

    def shards(slot_factors, slot_pairs, pivot_factors, a_factors, diag_factor, sketch):
        tile, rank = sketch.shape
        columns, rows = pivot_factors.shape[:2]
        slots = slot_factors.shape[2]
        chunk = tile // n_row
        vmem = pl.BlockSpec(memory_space=pltpu.VMEM)
        hbm = pl.BlockSpec(memory_space=pl.ANY)
        dma = pltpu.SemaphoreType.DMA
        out = jax.ShapeDtypeStruct((1, tile, rank), F32)
        n_chip = n_col // 2
        wide = jax.ShapeDtypeStruct((tile, rank), F32)
        sketched, solved, hinv = pl.pallas_call(
            functools.partial(kernel, n_row, n_col),
            out_shape=(wide, wide, jax.ShapeDtypeStruct((rank, rank), F32)),
            in_specs=[hbm, pl.BlockSpec(memory_space=pltpu.SMEM), vmem, hbm, hbm, hbm],
            out_specs=(vmem, vmem, vmem),
            scratch_shapes=[
                pltpu.VMEM(slot_factors.shape, BF16),
                pltpu.VMEM(a_factors.shape, BF16),
                pltpu.VMEM((tile, rank), F32),
                pltpu.VMEM((tile, tile), F32),
                pltpu.VMEM((tile // rank, rank, rank), F32),
                pltpu.VMEM((tile, tile), BF16),
                pltpu.VMEM((tile, tile), BF16),
                pltpu.VMEM((tile, columns * rank), BF16),
                pltpu.VMEM((n_row, tile, columns * rank), BF16),
                pltpu.VMEM((slots * rank, columns * rank), F32),
                pltpu.VMEM((tile, rank), F32),
                pltpu.VMEM((tile, rank), F32),
                pltpu.VMEM((n_row - 1, HALVES, chunk // HALVES, rank), F32),
                pltpu.VMEM((tile, rank), F32),
                pltpu.VMEM((n_row, columns * rank, rank), F32),
                pltpu.VMEM((rank, rank), F32),
                pltpu.VMEM(((slots + 1) * rank, rank), F32),
                dma(()), dma(()), dma(()), dma(()),
                dma((n_chip - 1,)), dma((n_chip - 1,)),
                dma((n_chip - 1,)), dma((n_chip - 1,)),
                dma((n_chip,)), dma((n_chip,)),
                dma((n_chip,)), dma((n_chip,)),
                dma((n_row - 1,)), dma((n_row - 1,)),
                dma((n_row - 1, n_chip - 1)), dma((n_row - 1, n_chip - 1)),
                dma((n_row - 1, n_chip)), dma((n_row - 1, n_chip)),
                dma((n_row - 1, HALVES)), dma((n_row - 1, HALVES)),
                dma((n_row - 1, HALVES)), dma((n_row - 1, HALVES)),
                dma((n_row - 1,)), dma((n_row - 1,)),
            ],
            compiler_params=pltpu.CompilerParams(
                collective_id=0, has_side_effects=True, vmem_limit_bytes=60 * 1024 * 1024
            ),
            cost_estimate=pl.CostEstimate(flops=4 * 10**9, bytes_accessed=8 * 10**6, transcendentals=0),
        )(slot_factors, slot_pairs, pivot_factors, a_factors, diag_factor, sketch)
        return pl.pallas_call(
            functools.partial(scale_kernel, float(tile) ** 0.5),
            out_shape=(out, out),
            in_specs=[vmem, vmem, vmem],
            out_specs=(vmem, vmem),
            compiler_params=pltpu.CompilerParams(vmem_limit_bytes=60 * 1024 * 1024),
        )(sketched, solved, hinv)

    in_specs = (
        P("row", "col", None, None, None),
        P("row", "col", None),
        P("row", "col", None),
        P("col", None, None),
        P(),
        P(),
    )
    out_specs = (P("col", None, None), P("col", None, None))
    return jax.shard_map(shards, mesh=mesh, in_specs=in_specs, out_specs=out_specs, check_vma=False)
```

```python
import functools

import jax
import jax.numpy as jnp
from jax import lax
from jax.experimental import pallas as pl
from jax.experimental.pallas import tpu as pltpu
from jax.sharding import PartitionSpec as P

HALVES = 2
MESH = pl.DeviceIdType.MESH
F32 = jnp.float32
BF16 = jnp.bfloat16
NN = (((1,), (0,)), ((), ()))
TN = (((0,), (0,)), ((), ()))
NT = (((1,), (1,)), ((), ()))


def split(x):
    high = x.astype(BF16)
    return high, (x - high.astype(F32)).astype(BF16)


def dot(a, b, dims=NN):
    return lax.dot_general(a, b, dims, preferred_element_type=F32)


def fold(x):
    width = x.shape[1] // 2
    return x[:, :width] + x[:, width:]


def dot_exact_left(a, b, dims=NN):
    return fold(dot(a, jnp.concatenate(split(b), axis=1), dims))


def dot_split(a, b, dims=NN):
    a_high, a_low = a
    b_high, b_low = b
    if dims == NT or b_high.shape[1] > 128:
        return dot(a_high, b_high, dims) + (dot(a_high, b_low, dims) + dot(a_low, b_high, dims))
    both = jnp.concatenate([b_high, b_low], axis=1)
    if dims == NN and b_high.shape[0] <= 128:
        return fold(dot(jnp.concatenate([a_high, a_low], axis=1), jnp.concatenate([both, both], axis=0)))
    return fold(dot(a_high, both, dims)) + dot(a_low, b_high, dims)


def dot_wide(a, b, dims=NN):
    return dot_split(split(a), split(b), dims)


def kernel(
    n_row, n_col,
    slot_hbm, pairs_ref, pivot_ref, a_hbm, diag_ref, sketch_hbm,
    sketched_ref, solved_ref, hinv_ref,
    slot_ref, a_ref, sketch_ref, diag_v, inv_small, inv_high, inv_low, pv_all, pu_all, coupling,
    y_own, y_part, y_in, y_full, x_all, gram_v, inner_v,
    slot_sem, a_sem, sketch_sem, diag_sem, pv_send, pv_recv, pu_send, pu_recv, sv_send, sv_recv, su_send, su_recv, pz_send, pz_recv,
    pf_send, pf_recv, sf_send, sf_recv, rs_send, rs_recv, ag_send, ag_recv, x_send, x_recv,
):
    tile, rank = sketch_ref.shape
    columns, rows = pivot_ref.shape[0], pivot_ref.shape[1]
    slots = slot_ref.shape[2]
    chunk = tile // n_row
    half = chunk // HALVES
    r = lax.axis_index("row")
    c = lax.axis_index("col")
    n_chip = n_col // 2
    core, chip = lax.rem(c, 2), lax.div(c, 2)
    sibling = c + 1 - 2 * core

    a_copy = pltpu.make_async_copy(a_hbm, a_ref, a_sem)
    sketch_copy = pltpu.make_async_copy(sketch_hbm, sketch_ref, sketch_sem)
    slot_copy = pltpu.make_async_copy(slot_hbm, slot_ref, slot_sem)
    diag_copy = pltpu.make_async_copy(diag_ref, diag_v, diag_sem)
    a_copy.start()
    sketch_copy.start()
    diag_copy.start()
    slot_copy.start()

    def piece(index):
        return pl.ds(pl.multiple_of(index * rows, rows), rows)

    def part(index, h):
        return pl.ds(pl.multiple_of(index * chunk + h * half, half), half)

    for j in range(columns):
        lanes = slice(j * rank, (j + 1) * rank)
        pu_all[r, piece(c), lanes] = pivot_ref[j, :, :rank]
        pv_all[piece(c), lanes] = pivot_ref[j, :, rank:]

    barrier = pltpu.get_barrier_semaphore()

    def chip_mate(e):
        return lax.rem(chip + e, n_chip) * 2 + core

    def chip_source(e):
        return lax.rem(chip + n_chip - e, n_chip) * 2 + core

    def sibling_source(e):
        return lax.rem(chip + n_chip - e, n_chip) * 2 + 1 - core

    def greet_chip(e, _):
        pl.semaphore_signal(barrier, inc=1, device_id={"col": chip_mate(e)}, device_id_type=MESH)
        return 0

    def greet_row(d, _):
        pl.semaphore_signal(barrier, inc=1, device_id={"row": lax.rem(r + d, n_row)}, device_id_type=MESH)
        return 0

    lax.fori_loop(1, n_chip, greet_chip, 0)
    lax.fori_loop(1, n_row, greet_row, 0)
    pl.semaphore_signal(barrier, inc=1, device_id={"col": sibling}, device_id_type=MESH)
    pl.semaphore_wait(barrier, n_chip - 1 + n_row - 1 + 1)

    def to_col(ref, send, recv, target):
        return pltpu.make_async_remote_copy(
            ref, ref, send, recv, device_id={"col": target}, device_id_type=MESH
        )

    def to_row(source, target, send, recv, d):
        return pltpu.make_async_remote_copy(
            source, target, send, recv, device_id={"row": lax.rem(r + d, n_row)}, device_id_type=MESH
        )

    def pv_copy(e, index):
        return to_col(pv_all.at[piece(index)], pv_send.at[e - 1], pv_recv.at[e - 1], chip_mate(e))

    def pu_copy(e, index):
        return to_col(pu_all.at[r, piece(index)], pu_send.at[e - 1], pu_recv.at[e - 1], chip_mate(e))

    def sv_copy(e, index):
        return to_col(pv_all.at[piece(index)], sv_send.at[e], sv_recv.at[e], sibling)

    def su_copy(e, index):
        return to_col(pu_all.at[r, piece(index)], su_send.at[e], su_recv.at[e], sibling)

    def pz_copy(d, index):
        ref = pu_all.at[index, piece(c)]
        return to_row(ref, ref, pz_send.at[d - 1], pz_recv.at[d - 1], d)

    def pf_copy(d, e, index):
        ref = pu_all.at[row_source(d), piece(index)]
        return to_col(ref, pf_send.at[d - 1, e - 1], pf_recv.at[d - 1, e - 1], chip_mate(e))

    def sf_copy(d, e, index):
        ref = pu_all.at[row_source(d), piece(index)]
        return to_col(ref, sf_send.at[d - 1, e], sf_recv.at[d - 1, e], sibling)

    def rs_copy(d, h):
        return to_row(
            y_part.at[part(lax.rem(r + d, n_row), h)], y_in.at[d - 1, h],
            rs_send.at[d - 1, h], rs_recv.at[d - 1, h], d,
        )

    def ag_copy(d, index, h):
        ref = y_full.at[part(index, h)]
        return to_row(ref, ref, ag_send.at[d - 1, h], ag_recv.at[d - 1, h], d)

    def x_copy(d, index):
        ref = x_all.at[index]
        return to_row(ref, ref, x_send.at[d - 1], x_recv.at[d - 1], d)

    def row_source(d):
        return lax.rem(r + n_row - d, n_row)

    def each(n, act):
        def body(d, _):
            act(d)
            return 0

        lax.fori_loop(1, n, body, 0)

    def push_pivots(e):
        pv_copy(e, c).start()
        pu_copy(e, c).start()

    each(n_chip, push_pivots)
    sv_copy(0, c).start()
    su_copy(0, c).start()
    each(n_row, lambda d: pz_copy(d, r).start())

    sketch_copy.wait()
    a_copy.wait()
    sketch_split = split(sketch_ref[...])
    a_left = a_ref[0, :, :rank]
    a_right = a_ref[0, :, rank:]
    a_sketch = dot(a_right, sketch_split[0], TN) + dot(a_right, sketch_split[1], TN)
    y_own[...] = dot_exact_left(a_left, a_sketch)

    def pass_pivots(e):
        pv_copy(e, chip_source(e)).wait_recv()
        sv_copy(e, chip_source(e)).start()
        pu_copy(e, chip_source(e)).wait_recv()
        su_copy(e, chip_source(e)).start()

    diag_copy.wait()
    blocks = tile // rank
    sub = lax.broadcasted_iota(jnp.int32, (rank, rank), 0)
    lane = lax.broadcasted_iota(jnp.int32, (rank, rank), 1)
    on_diag = sub == lane

    def diag_block(b):
        span = slice(b * rank, (b + 1) * rank)
        return diag_v[span, span]

    for b in range(blocks):
        low = diag_block(b)
        only = jnp.where(on_diag, low, 0.0)
        inv_sub = 1.0 / jnp.sum(only, axis=1, keepdims=True)
        inv_lane = 1.0 / jnp.sum(only, axis=0, keepdims=True)
        pair = (sub == lane + 1) & ((lane & 1) == 0)
        inv_small[b] = jnp.where(on_diag, inv_lane, 0.0) - jnp.where(pair, low * inv_sub * inv_lane, 0.0)

    def double(level, _):
        step = (lax.shift_right_logical(sub, level + 1) == lax.shift_right_logical(lane, level + 1)) & (
            lax.shift_right_logical(sub, level) != lax.shift_right_logical(lane, level)
        )
        for b in range(blocks):
            now = inv_small[b]
            now_split = split(now)
            cross = split(jnp.where(step, diag_block(b), 0.0))
            inv_small[b] = now - dot_split(split(dot_split(now_split, cross)), now_split)
        return 0

    levels = rank.bit_length() - 1
    early = 3
    each(n_chip, pass_pivots)
    lax.fori_loop(1, early, double, 0)
    slot_copy.wait()

    def take_pivots(e):
        sv_copy(e, sibling_source(e)).wait_recv()
        su_copy(e, sibling_source(e)).wait_recv()

    take_pivots(0)
    each(n_chip, take_pivots)
    pivot_right = pv_all[...]
    for s in range(slots):
        code = pairs_ref[0, 0, s]
        coupled = dot(slot_ref[0, 0, s, :, rank:], pivot_right, TN)
        for j in range(columns):
            lanes = slice(j * rank, (j + 1) * rank)
            coupling[s * rank:(s + 1) * rank, lanes] = jnp.where(code == j, coupled[:, lanes], 0.0)
    pivot_left = pu_all[r]
    weights = dot(pivot_left, sketch_split[0], TN) + dot(pivot_left, sketch_split[1], TN)
    mixed = dot_wide(coupling[...], weights)
    mixed_split = split(mixed)

    def update_rows(index, h):
        span = part(index, h)
        total = jnp.zeros((half, rank), F32)
        for s in range(slots):
            left = slot_ref[0, 0, s, span, :rank]
            for term in mixed_split:
                total += dot(left, term[s * rank:(s + 1) * rank])
        y_part[span] = total

    def push_update(d, h):
        update_rows(lax.rem(r + d, n_row), h)
        rs_copy(d, h).start()

    for h in range(HALVES):
        each(n_row, lambda d: push_update(d, h))
    for h in range(HALVES):
        update_rows(r, h)

    def forward(d):
        pz_copy(d, row_source(d)).wait_recv()
        each(n_chip, lambda e: pf_copy(d, e, c).start())
        sf_copy(d, 0, c).start()

    each(n_row, forward)

    lax.fori_loop(early, levels, double, 0)

    for h in range(HALVES):
        each(n_row, lambda d: rs_copy(d, h).wait_recv())
        mine = y_own[part(r, h)] - y_part[part(r, h)]
        for d in range(1, n_row):
            mine = mine - y_in[d - 1, h]
        y_full[part(r, h)] = mine
        each(n_row, lambda d: ag_copy(d, r, h).start())

    def pass_forward(d, e):
        pf_copy(d, e, chip_source(e)).wait_recv()
        sf_copy(d, e, chip_source(e)).start()

    each(n_row, lambda d: each(n_chip, lambda e: pass_forward(d, e)))

    def products(index, h):
        span = part(index, h)
        halves = split(y_full[span])
        lefts = [slot_ref[0, 0, s, span, :rank] for s in range(slots)] + [a_ref[0, span, :rank]]
        whole = fold(dot(jnp.concatenate([*lefts, *halves], axis=1), jnp.concatenate(halves, axis=1), TN))
        edge = (slots + 1) * rank
        return whole[:edge], whole[edge:edge + rank] + whole[edge + rank:]

    inner_v[...] = jnp.zeros_like(inner_v)
    gram_v[...] = jnp.zeros_like(gram_v)

    def add_products(index, h):
        inner, gram = products(index, h)
        inner_v[...] += inner
        gram_v[...] += gram

    for h in range(HALVES):
        add_products(r, h)

    inv_high[...] = jnp.zeros_like(inv_high)
    inv_low[...] = jnp.zeros_like(inv_low)
    for b in range(blocks):
        span = slice(b * rank, (b + 1) * rank)
        high, low = split(inv_small[b])
        inv_high[span, span] = high
        inv_low[span, span] = low
    size = rank
    while size < tile:
        for start in range(0, tile, 2 * size):
            first = slice(start, start + size)
            second = slice(start + size, start + 2 * size)
            middle = dot_split(split(diag_v[second, first]), (inv_high[first, first], inv_low[first, first]))
            cross = dot_split((inv_high[second, second], inv_low[second, second]), split(middle))
            high, low = split(-cross)
            inv_high[second, first] = high
            inv_low[second, first] = low
        size *= 2

    def take_chunk(d, h):
        ag_copy(d, row_source(d), h).wait_recv()
        add_products(row_source(d), h)

    for h in range(HALVES):
        each(n_row, lambda d: take_chunk(d, h))
    x_all[r] = dot_wide(coupling[...], inner_v[:slots * rank], TN)
    each(n_row, lambda d: x_copy(d, r).start())
    sketched_ref[...] = y_full[...]
    solved_ref[...] = dot_exact_left(a_right, inner_v[slots * rank:]) - dot_exact_left(pu_all[r], x_all[r])

    state_gram, state_eye = gram_v[...], jnp.where(on_diag, 1.0, 0.0)
    group = 16
    sub_group = lax.broadcasted_iota(jnp.int32, (group, rank), 0)
    lane_group = lax.broadcasted_iota(jnp.int32, (group, rank), 1)
    for start in range(0, rank, group):
        block = state_gram[start:start + group]
        eye = state_eye[start:start + group]
        cols = [
            jnp.broadcast_to(block[:, start + u:start + u + 1], (group, rank)) for u in range(group)
        ]
        pivots = jnp.zeros((group, rank), F32)
        for t in range(group):
            pivot = cols[t][t:t + 1]
            pivots = jnp.where(sub_group == t, pivot, pivots)
            if t + 1 < group:
                factor = jnp.where(sub_group > t, cols[t] * (1.0 / pivot), 0.0)
                for u in range(t + 1, group):
                    cols[u] = cols[u] - factor * cols[u][t:t + 1]
                block = block - factor * block[t:t + 1]
                eye = eye - factor * eye[t:t + 1]
        scale = lax.rsqrt(pivots)
        block = block * scale
        eye = eye * scale
        hinv_ref[start:start + group] = eye
        if start + group < rank:
            left_high, left_low = split(jnp.where(lane_group >= start + group, block, 0.0))
            block_high, block_low = split(block)
            eye_high, eye_low = split(eye)
            left = jnp.concatenate([left_high, left_high, left_low, left_low], axis=0)
            state_gram = state_gram - dot(
                left, jnp.concatenate([block_high, block_low, block_high, block_low], axis=0), TN
            )
            state_eye = state_eye - dot(
                left, jnp.concatenate([eye_high, eye_low, eye_high, eye_low], axis=0), TN
            )

    def take_product(d):
        sf_copy(d, 0, sibling_source(0)).wait_recv()
        each(n_chip, lambda e: sf_copy(d, e, sibling_source(e)).wait_recv())
        x_copy(d, row_source(d)).wait_recv()
        solved_ref[...] -= dot_exact_left(pu_all[row_source(d)], x_all[row_source(d)])

    each(n_row, take_product)
    high, low = split(solved_ref[...])
    band = 2 * rank
    for start in range(0, tile, band):
        span, upto = slice(start, start + band), slice(0, start + band)
        solved_ref[span] = dot_split((inv_high[span, upto], inv_low[span, upto]), (high[upto], low[upto]))

    def finish_chip(e):
        pv_copy(e, c).wait_send()
        pu_copy(e, c).wait_send()

    def finish_sibling(e):
        sv_copy(e, chip_source(e)).wait_send()
        su_copy(e, chip_source(e)).wait_send()

    def finish_row(d):
        pz_copy(d, r).wait_send()
        for h in range(HALVES):
            rs_copy(d, h).wait_send()
            ag_copy(d, r, h).wait_send()
        x_copy(d, r).wait_send()
        sf_copy(d, 0, c).wait_send()

    def finish_forward(d, e):
        pf_copy(d, e, c).wait_send()
        sf_copy(d, e, chip_source(e)).wait_send()

    each(n_chip, finish_chip)
    finish_sibling(0)
    each(n_chip, finish_sibling)
    each(n_row, finish_row)
    each(n_row, lambda d: each(n_chip, lambda e: finish_forward(d, e)))


def scale_kernel(root, sketched_ref, solved_ref, hinv_ref, basis_ref, coeff_ref):
    factor = split(hinv_ref[...])
    basis_ref[0] = dot_split(split(sketched_ref[...]), factor, NT) * root
    coeff_ref[0] = dot_split(split(solved_ref[...]), factor, NT) * (1.0 / root)


def solution(mesh):
    n_row, n_col = mesh.shape["row"], mesh.shape["col"]

    def shards(slot_factors, slot_pairs, pivot_factors, a_factors, diag_factor, sketch):
        tile, rank = sketch.shape
        columns, rows = pivot_factors.shape[:2]
        slots = slot_factors.shape[2]
        chunk = tile // n_row
        vmem = pl.BlockSpec(memory_space=pltpu.VMEM)
        hbm = pl.BlockSpec(memory_space=pl.ANY)
        dma = pltpu.SemaphoreType.DMA
        out = jax.ShapeDtypeStruct((1, tile, rank), F32)
        n_chip = n_col // 2
        wide = jax.ShapeDtypeStruct((tile, rank), F32)
        sketched, solved, hinv = pl.pallas_call(
            functools.partial(kernel, n_row, n_col),
            out_shape=(wide, wide, jax.ShapeDtypeStruct((rank, rank), F32)),
            in_specs=[hbm, pl.BlockSpec(memory_space=pltpu.SMEM), vmem, hbm, hbm, hbm],
            out_specs=(vmem, vmem, vmem),
            scratch_shapes=[
                pltpu.VMEM(slot_factors.shape, BF16),
                pltpu.VMEM(a_factors.shape, BF16),
                pltpu.VMEM((tile, rank), F32),
                pltpu.VMEM((tile, tile), F32),
                pltpu.VMEM((tile // rank, rank, rank), F32),
                pltpu.VMEM((tile, tile), BF16),
                pltpu.VMEM((tile, tile), BF16),
                pltpu.VMEM((tile, columns * rank), BF16),
                pltpu.VMEM((n_row, tile, columns * rank), BF16),
                pltpu.VMEM((slots * rank, columns * rank), F32),
                pltpu.VMEM((tile, rank), F32),
                pltpu.VMEM((tile, rank), F32),
                pltpu.VMEM((n_row - 1, HALVES, chunk // HALVES, rank), F32),
                pltpu.VMEM((tile, rank), F32),
                pltpu.VMEM((n_row, columns * rank, rank), F32),
                pltpu.VMEM((rank, rank), F32),
                pltpu.VMEM(((slots + 1) * rank, rank), F32),
                dma(()), dma(()), dma(()), dma(()),
                dma((n_chip - 1,)), dma((n_chip - 1,)),
                dma((n_chip - 1,)), dma((n_chip - 1,)),
                dma((n_chip,)), dma((n_chip,)),
                dma((n_chip,)), dma((n_chip,)),
                dma((n_row - 1,)), dma((n_row - 1,)),
                dma((n_row - 1, n_chip - 1)), dma((n_row - 1, n_chip - 1)),
                dma((n_row - 1, n_chip)), dma((n_row - 1, n_chip)),
                dma((n_row - 1, HALVES)), dma((n_row - 1, HALVES)),
                dma((n_row - 1, HALVES)), dma((n_row - 1, HALVES)),
                dma((n_row - 1,)), dma((n_row - 1,)),
            ],
            compiler_params=pltpu.CompilerParams(
                collective_id=0, has_side_effects=True, vmem_limit_bytes=60 * 1024 * 1024
            ),
            cost_estimate=pl.CostEstimate(flops=4 * 10**9, bytes_accessed=8 * 10**6, transcendentals=0),
        )(slot_factors, slot_pairs, pivot_factors, a_factors, diag_factor, sketch)
        return pl.pallas_call(
            functools.partial(scale_kernel, float(tile) ** 0.5),
            out_shape=(out, out),
            in_specs=[vmem, vmem, vmem],
            out_specs=(vmem, vmem),
            compiler_params=pltpu.CompilerParams(vmem_limit_bytes=60 * 1024 * 1024),
        )(sketched, solved, hinv)

    in_specs = (
        P("row", "col", None, None, None),
        P("row", "col", None),
        P("row", "col", None),
        P("col", None, None),
        P(),
        P(),
    )
    out_specs = (P("col", None, None), P("col", None, None))
    return jax.shard_map(shards, mesh=mesh, in_specs=in_specs, out_specs=out_specs, check_vma=False)
```
